32 devices in a mesh: groups: 2 (over y), strip: 16 (over z, x, core).
Axes of the slice: x: 2, y: 2, z: 4, core: 2. Of those that a mesh axis runs over, the one named last changes fastest.
Arguments:
- data: bfloat16 [512, 128, 256], P(('groups', 'strip')), parts along dimension 0, may hold values from -6 to 6
- response: bfloat16 [256, 256], replicated
- pixel_ids: int32 [256], replicated, may hold values from 0 to 255, each once
- shift_bins: int32 [2, 256], replicated, may hold values from -64 to 64, as said below
Outputs:
- aligned: bfloat16 [256, 512, 128], P('strip', 'groups'), parts along dimension 1
- image_sum: float32 [512, 128], P(('groups', 'strip')), parts along dimension 0
- correlation: float32 [512, 81], P(('groups', 'strip')), parts along dimension 0
The draws below stay inside these ranges and needn't reach their ends.
There are 2 independent parts, one for each index of `groups`. The reference program is written for one: setup_inputs(seed, part) draws one part's arguments, and reference() takes and returns one part's arrays. A program takes and returns all parts, laid end to end along the dimension named above; an argument that names none is the same for every part. Nothing has to cross between parts.
Inputs may be any that keep to these rules, and one draw needn't show every extreme that they name: `shift_bins`: every value in [-64, 64] may occur; both ends occur in each row.
All inputs are finite; a program needn't handle non-finite values.
Results may differ from the reference program's by a relative error of at most 0.0072.
Values may be sent and summed in bfloat16 or wider, within the bound.
A program may use at most 128 MiB of HBM per device.

```python
import jax
import jax.numpy as jnp
from jax import lax

K = 256
SX = 128
HALO = 16
LAGS = 4
SY = 256


def draw_response(key, part):
    noise = jax.random.normal(jax.random.fold_in(key, 11), (K, K), jnp.float32)
    matrix = jnp.eye(K, dtype=jnp.float32) + noise * (0.5 / jnp.sqrt(jnp.float32(K)))
    return matrix.astype(jnp.bfloat16)


def draw_shift_bins(key, part):
    values = jax.random.randint(jax.random.fold_in(key, 21), (2, K), -4 * HALO, 4 * HALO + 1)
    order = jax.random.permutation(jax.random.fold_in(key, 22), K)
    values = values.at[:, order[0]].set(-4 * HALO)
    values = values.at[:, order[1]].set(4 * HALO)
    return values.astype(jnp.int32)


def block_scale(own_key, shape, split, least, high):
    def one(dim, shards_of):
        draws = jax.random.uniform(jax.random.fold_in(jax.random.fold_in(own_key, 6), dim), (shards_of,), jnp.float32, least / len(split), high / len(split))
        return jnp.repeat(jnp.exp(draws), shape[dim] // shards_of).reshape((-1,) + (1,) * (len(shape) - dim - 1))

    factor_of = one(*split[0])
    for cut in split[1:]:
        factor_of = factor_of * one(*cut)
    return factor_of


def gaussian(stream_key, shape, spread, bound, shards=(), kind=jnp.bfloat16):
    array = spread * jax.random.normal(stream_key, shape, jnp.float32)
    if shards:
        array = array * block_scale(stream_key, shape, shards, -0.22, 0.18)
    return jnp.clip(array, -bound, bound).astype(kind)


def setup_inputs(seed: int = 0, part: int = 0) -> dict:
    key_list = jax.random.split(jax.random.key(seed), 5)
    part_keys = jax.random.split(jax.random.fold_in(key_list[4], part), 5)
    data = gaussian(part_keys[0], (SY, SX, K), 1.0, 6.0, ((0, 16),))
    response = draw_response(jax.random.fold_in(key_list[4], 71), part)
    pixel_ids = jax.random.permutation(key_list[2], K).astype(jnp.int32)
    shift_bins = draw_shift_bins(jax.random.fold_in(key_list[4], 71), part)
    return dict(data=data, response=response, pixel_ids=pixel_ids, shift_bins=shift_bins)


def tap_weights(shift_bins):
    offsets = jnp.arange(-HALO, HALO + 1).astype(jnp.float32)
    shifted = offsets[None, None, :] - shift_bins[:, :, None].astype(jnp.float32) / 4.0
    kernel = jnp.sinc(shifted) * (0.5 + 0.5 * jnp.cos(jnp.pi * shifted / (HALO + 1)))
    return jnp.where(jnp.abs(shifted) < HALO + 1, kernel, 0.0).astype(jnp.bfloat16)

def tap_sum(image, weights, axis):
    length = image.shape[axis]
    widths = [(0, 0), (0, 0)]
    widths[axis] = (HALO, HALO)
    padded = jnp.pad(image, widths)
    running = jnp.zeros(image.shape, jnp.float32)
    for index in range(2 * HALO + 1):
        offset = 2 * HALO - index
        section = lax.slice_in_dim(padded, offset, offset + length, axis=axis)
        running = running + weights[index].astype(jnp.float32) * section.astype(jnp.float32)
    return running.astype(jnp.bfloat16)

def shift_image(image, row_weights, col_weights):
    return tap_sum(tap_sum(image, row_weights, 0), col_weights, 1)

def reference(data, response, pixel_ids, shift_bins):
    chosen = jnp.take(response, pixel_ids, axis=1)
    corrected = jnp.dot(data.reshape(SY * SX, K), chosen, preferred_element_type=jnp.float32)
    corrected = corrected.astype(jnp.bfloat16).reshape(SY, SX, K).transpose(2, 0, 1)
    weights = tap_weights(shift_bins)
    aligned = lax.map(lambda items: shift_image(items[0], items[1], items[2]), (corrected, weights[0], weights[1]))
    image_sum = lax.optimization_barrier(jnp.sum(aligned, axis=0, dtype=jnp.float32))
    ref_pad = jnp.pad(image_sum.astype(jnp.bfloat16), LAGS)
    flattened = aligned.reshape(K, SY * SX)
    columns = []
    for lag_row in range(2 * LAGS + 1):
        windows = jnp.stack([ref_pad[lag_row:lag_row + SY, lag_col:lag_col + SX] for lag_col in range(2 * LAGS + 1)])
        windows = windows.reshape(2 * LAGS + 1, SY * SX)
        columns.append(lax.dot_general(flattened, windows, (((1,), (1,)), ((), ())), preferred_element_type=jnp.float32))
    correlation = jnp.concatenate(columns, axis=1) / jnp.sqrt(jnp.float32(K * SY * SX))
    return (aligned, image_sum, correlation)
```

```python
import functools
import math

import jax
import jax.numpy as jnp
from jax import lax
from jax.experimental import pallas as pl
from jax.experimental.pallas import tpu as pltpu
from jax.sharding import PartitionSpec as P

HALO = 16
LAGS = 4
TAPS = 2 * HALO + 1
WIDE = 2 * LAGS + 1
SUB = 8
MESH = pl.DeviceIdType.MESH


def tap_value(offset, bins):
    u = offset.astype(jnp.float32) - bins.astype(jnp.float32) / 4.0
    angle = jnp.pi * u
    safe = jnp.where(u == 0.0, 1.0, angle)
    sinc = jnp.where(u == 0.0, 1.0, jnp.sin(safe) / safe)
    value = sinc * (0.5 + 0.5 * jnp.cos(angle / (HALO + 1)))
    inside = (jnp.abs(u) < HALO + 1) & (jnp.abs(offset) <= HALO)
    return jnp.where(inside, value, 0.0).astype(jnp.bfloat16)


def kernel(
    n, chunks, scaling,
    data_ref, resp_ref, ids_ref, bins_ref, bins_smem,
    aligned_ref, sum_ref, corr_out_ref,
    spread, natural, corrected, received, row_bands, col_bands,
    row_table, row_taps, col_taps, totals, halo_out, halo_in, image, image_pad, image_t, diagonals,
    send_sems, recv_sems, halo_send, halo_recv, image_send, image_recv, own_sem,
):
    rows, cols, pixels = data_ref.shape
    part = pixels // n
    size = part // chunks
    height = n * rows
    block = min(128, height)
    reach = rows + 2 * HALO
    me = lax.axis_index("strip")

    barrier = pltpu.get_barrier_semaphore()

    def greet(t, carry):
        other = lax.rem(me + t, n)
        pl.semaphore_signal(barrier, inc=1, device_id={"strip": other}, device_id_type=MESH)
        return carry

    lax.fori_loop(1, n, greet, 0)

    pick = lax.broadcasted_iota(jnp.int32, (pixels, pixels), 0) == ids_ref[...]
    chosen = jnp.dot(
        resp_ref[...], pick.astype(jnp.float32).astype(jnp.bfloat16), preferred_element_type=jnp.float32
    )
    chosen_t = chosen.T.astype(jnp.bfloat16)
    for y in range(rows):
        row = lax.dot_general(
            chosen_t, data_ref[y], (((1,), (1,)), ((), ())), preferred_element_type=jnp.float32
        )
        natural[y] = row.astype(jnp.bfloat16)
        spread[pl.ds(y, pixels, stride=rows), :] = row
    corrected[...] = spread[...].reshape(pixels, rows, cols).astype(jnp.bfloat16)

    pl.semaphore_wait(barrier, n - 1)

    def strip_copy(chunk, other, owner, sender):
        return pltpu.make_async_remote_copy(
            src_ref=corrected.at[pl.ds(owner * part + chunk * size, size)],
            dst_ref=received.at[
                pl.ds(chunk * size, size), pl.ds(pl.multiple_of(HALO + sender * rows, HALO), rows)
            ],
            send_sem=send_sems.at[chunk, other],
            recv_sem=recv_sems.at[chunk, sender],
            device_id={"strip": other},
            device_id_type=MESH,
        )

    def partner(step):
        half = lax.div(step + 1, 2)
        far = n // 2 + jnp.where(lax.rem(step, 2) == 0, half, -half)
        return lax.rem(me + far, n)

    def send_chunk(chunk):
        def one(step, carry):
            other = partner(step)
            strip_copy(chunk, other, other, me).start()
            return carry

        lax.fori_loop(0, n - 1, one, 0)

    first_sent = (chunks + 1) // 2
    for chunk in range(first_sent):
        send_chunk(chunk)
    own_copy = pltpu.make_async_copy(
        corrected.at[pl.ds(me * part, part)],
        received.at[:, pl.ds(pl.multiple_of(HALO + me * rows, HALO), rows)],
        own_sem,
    )
    own_copy.start()

    taps_at = lax.broadcasted_iota(jnp.int32, (reach + rows, pixels), 0)
    row_table[...] = tap_value(taps_at - (rows - 1) - HALO, bins_ref[0:1, :]).astype(jnp.float32)
    for y in range(rows):
        row_taps[y] = row_table[pl.ds(rows - 1 - y, reach), :].astype(jnp.bfloat16)
    for j in range(TAPS):
        offset = jnp.full((1, pixels), j - HALO, jnp.int32)
        tap = tap_value(offset, bins_ref[1:2, :]).astype(jnp.float32)
        col_taps[j] = jnp.broadcast_to(tap, (16, pixels)).astype(jnp.bfloat16)
    totals[...] = jnp.zeros_like(totals)

    def add_row(y, carry):
        taps = row_taps[y].reshape(1, reach // 16, 16, pixels)
        outer = (taps * col_taps[...].reshape(TAPS, 1, 16, pixels)).reshape(TAPS * reach, pixels)
        totals[...] += jnp.dot(outer, natural[y], preferred_element_type=jnp.float32)
        return carry

    lax.fori_loop(0, rows, add_row, 0)
    lane = lax.broadcasted_iota(jnp.int32, (reach, cols), 1)
    share = jnp.zeros((reach, cols), jnp.float32)
    for j in range(TAPS):
        shift = j - HALO
        moved = totals[pl.ds(j * reach, reach), :]
        if shift:
            moved = pltpu.roll(moved, shift % cols, 1)
            source = lane - shift
            moved = jnp.where((source >= 0) & (source < cols), moved, 0.0)
        share = share + moved
    halo_out[...] = share

    before, after = lax.rem(me + n - 1, n), lax.rem(me + 1, n)

    def halo_copy(side, other, start):
        return pltpu.make_async_remote_copy(
            src_ref=halo_out.at[pl.ds(start, HALO)],
            dst_ref=halo_in.at[side],
            send_sem=halo_send.at[side],
            recv_sem=halo_recv.at[side],
            device_id={"strip": other},
            device_id_type=MESH,
        )

    to_after = halo_copy(0, after, HALO + rows)
    to_before = halo_copy(1, before, 0)
    to_after.start()
    to_before.start()
    for chunk in range(first_sent, chunks):
        if chunk == chunks - 1:
            break
        send_chunk(chunk)
    to_after.wait_recv()
    to_before.wait_recv()
    mine = halo_out[pl.ds(HALO, rows), :]
    fill = jnp.zeros((rows - HALO, cols), jnp.float32)
    from_before = jnp.where(me > 0, halo_in[0], 0.0)
    from_after = jnp.where(me < n - 1, halo_in[1], 0.0)
    if rows > HALO:
        from_before = jnp.concatenate([from_before, fill], axis=0)
        from_after = jnp.concatenate([fill, from_after], axis=0)
    mine = mine + from_before + from_after
    sum_ref[...] = mine
    image[pl.ds(pl.multiple_of(me * rows, HALO), rows), :] = mine.astype(jnp.bfloat16)

    def image_copy(other, sender):
        place = pl.ds(pl.multiple_of(sender * rows, HALO), rows)
        return pltpu.make_async_remote_copy(
            src_ref=image.at[place],
            dst_ref=image.at[place],
            send_sem=image_send.at[other],
            recv_sem=image_recv.at[sender],
            device_id={"strip": other},
            device_id_type=MESH,
        )

    def send_image(step, carry):
        image_copy(partner(step), me).start()
        return carry

    lax.fori_loop(0, n - 1, send_image, 0)
    if chunks > first_sent:
        send_chunk(chunks - 1)

    band_lane = lax.broadcasted_iota(jnp.int32, (1, 2 * block), 1)
    col_lane = lax.broadcasted_iota(jnp.int32, (1, cols), 1)
    col_offset = jnp.where(col_lane < cols // 2, col_lane, col_lane - cols)
    square = (cols, cols)
    near = (
        jnp.abs(lax.broadcasted_iota(jnp.int32, square, 0) - lax.broadcasted_iota(jnp.int32, square, 1))
        <= HALO
    )

    def bands(i, carry):
        pixel = me * part + i
        row_line = tap_value(HALO - band_lane, bins_smem[0, pixel]).astype(jnp.float32)
        row_band = jnp.broadcast_to(row_line, (block, 2 * block))
        row_bands[i] = pltpu.roll(row_band, 0, 1, stride=1, stride_axis=0).astype(jnp.bfloat16)
        col_line = tap_value(col_offset, bins_smem[1, pixel]).astype(jnp.float32)
        col_band = jnp.broadcast_to(col_line, square)
        col_band = pltpu.roll(col_band, 0, 1, stride=1, stride_axis=0)
        col_bands[i] = jnp.where(near, col_band, 0.0).astype(jnp.bfloat16)
        return carry

    lax.fori_loop(0, part, bands, 0)
    edge = jnp.zeros((part, HALO, cols), jnp.bfloat16)
    received[:, pl.ds(0, HALO), :] = edge
    received[:, pl.ds(HALO + height, HALO), :] = edge

    def await_image(step, carry):
        other = lax.rem(me + step, n)
        image_copy(other, other).wait_recv()
        return carry

    lax.fori_loop(1, n, await_image, 0)
    image_pad[pl.ds(0, SUB), :] = jnp.zeros((SUB, cols), jnp.float32)
    image_pad[pl.ds(SUB + height, SUB), :] = jnp.zeros((SUB, cols), jnp.float32)
    image_pad[pl.ds(SUB, height), :] = image[...].astype(jnp.float32)
    for a in range(WIDE):
        window = image_pad[pl.ds(SUB + a - LAGS, height), :]
        image_t[pl.ds(a * cols, cols), :] = window.T.astype(jnp.bfloat16)

    own_copy.wait()
    low_lane = lax.broadcasted_iota(jnp.int32, (SUB, cols), 1) < cols // 2
    tail_lane = lax.broadcasted_iota(jnp.int32, (SUB, cols), 1)
    tail_keep = (tail_lane < SUB) | (tail_lane >= cols // 2)
    pieces = cols // SUB

    def work_chunk(chunk, carry):
        def await_strip(step, inner):
            other = lax.rem(me + step, n)
            strip_copy(chunk, other, other, other).wait_recv()
            return inner

        lax.fori_loop(1, n, await_strip, 0)

        def pair(index, inner):
            first = chunk * size + 2 * index
            images = []
            for k in range(2):
                i = first + k
                row_band = row_bands[i][:, : block + 2 * HALO]
                col_band = col_bands[i]
                parts = []
                for start in range(0, height, block):
                    window = received[i, pl.ds(start, block + 2 * HALO), :]
                    moved = jnp.dot(row_band, window, preferred_element_type=jnp.float32)
                    moved = jnp.dot(
                        moved.astype(jnp.bfloat16), col_band, preferred_element_type=jnp.float32
                    ).astype(jnp.bfloat16)
                    aligned_ref[i, pl.ds(start, block), :] = moved
                    parts.append(moved)
                images.append(jnp.concatenate(parts, axis=0))
            both = jnp.concatenate(images, axis=1)
            for a in range(WIDE):
                products = jnp.dot(
                    image_t[pl.ds(a * cols, cols), :], both, preferred_element_type=jnp.float32
                )
                for k in range(2):
                    total = None
                    for piece in range(pieces):
                        term = products[piece * SUB : (piece + 1) * SUB, k * cols : (k + 1) * cols]
                        if piece:
                            term = pltpu.roll(term, cols - piece * SUB, 1)
                        if piece == 0:
                            term = jnp.where(low_lane, term, 0.0)
                        elif piece == pieces - 1:
                            term = jnp.where(tail_keep, term, 0.0)
                        total = term if total is None else total + term
                    place = pl.multiple_of((a * part + first + k) * SUB, SUB)
                    diagonals[pl.ds(place, SUB), :] = total
            return inner

        lax.fori_loop(0, size // 2, pair, 0)
        return carry

    lax.fori_loop(0, chunks, work_chunk, 0)

    gathered = jnp.zeros((WIDE * part, cols), jnp.float32)
    lane_in = lax.broadcasted_iota(jnp.int32, square, 0)
    lane_out = lax.broadcasted_iota(jnp.int32, square, 1)
    for s in range(SUB):
        wanted = s - (lane_out - LAGS)
        wanted = jnp.where(wanted < 0, wanted + cols, wanted)
        choose = ((lane_in == wanted) & (lane_out < WIDE)).astype(jnp.float32)
        gathered = gathered + jnp.dot(
            diagonals[pl.ds(s, WIDE * part, stride=SUB), :],
            choose,
            precision=lax.Precision.HIGHEST,
            preferred_element_type=jnp.float32,
        )
    result = jnp.zeros((part, cols), jnp.float32)
    for a in range(WIDE):
        lags = gathered[a * part : (a + 1) * part, :]
        result = result + (pltpu.roll(lags, a * WIDE, 1) if a else lags)
    corr_out_ref[...] = (result * scaling)[:, : WIDE * WIDE]

    def drain(step, carry):
        other = lax.rem(me + step, n)
        for chunk in range(chunks):
            strip_copy(chunk, other, other, me).wait_send()
        image_copy(other, me).wait_send()
        return carry

    lax.fori_loop(1, n, drain, 0)
    to_after.wait_send()
    to_before.wait_send()


def on_device(data, response, pixel_ids, shift_bins):
    rows, cols, pixels = data.shape
    n = lax.axis_size("strip")
    part = pixels // n
    chunks = max(1, part // 4)
    height = n * rows
    block = min(128, height)
    reach = rows + 2 * HALO
    assert rows >= HALO and (part // chunks) % 2 == 0 and height % block == 0
    scaling = 1.0 / math.sqrt(pixels * height * cols)
    vmem = pl.BlockSpec(memory_space=pltpu.VMEM)
    bf16, f32 = jnp.bfloat16, jnp.float32
    return pl.pallas_call(
        functools.partial(kernel, n, chunks, scaling),
        out_shape=(
            jax.ShapeDtypeStruct((part, height, cols), bf16),
            jax.ShapeDtypeStruct((rows, cols), f32),
            jax.ShapeDtypeStruct((part, WIDE * WIDE), f32),
        ),
        in_specs=[vmem] * 4 + [pl.BlockSpec(memory_space=pltpu.SMEM)],
        out_specs=(vmem, vmem, vmem),
        scratch_shapes=[
            pltpu.VMEM((pixels * rows, cols), f32),
            pltpu.VMEM((rows, pixels, cols), bf16),
            pltpu.VMEM((pixels, rows, cols), bf16),
            pltpu.VMEM((part, height + 2 * HALO, cols), bf16),
            pltpu.VMEM((part, block, 2 * block), bf16),
            pltpu.VMEM((part, cols, cols), bf16),
            pltpu.VMEM((reach + rows, pixels), f32),
            pltpu.VMEM((rows, reach, pixels), bf16),
            pltpu.VMEM((TAPS, 16, pixels), bf16),
            pltpu.VMEM((TAPS * reach, cols), f32),
            pltpu.VMEM((reach, cols), f32),
            pltpu.VMEM((2, HALO, cols), f32),
            pltpu.VMEM((height, cols), bf16),
            pltpu.VMEM((height + 2 * SUB, cols), f32),
            pltpu.VMEM((WIDE * cols, height), bf16),
            pltpu.VMEM((WIDE * part * SUB, cols), f32),
            pltpu.SemaphoreType.DMA((chunks, n)),
            pltpu.SemaphoreType.DMA((chunks, n)),
            pltpu.SemaphoreType.DMA((2,)),
            pltpu.SemaphoreType.DMA((2,)),
            pltpu.SemaphoreType.DMA((n,)),
            pltpu.SemaphoreType.DMA((n,)),
            pltpu.SemaphoreType.DMA(()),
        ],
        compiler_params=pltpu.CompilerParams(
            collective_id=0, has_side_effects=True, vmem_limit_bytes=48 * 1024 * 1024
        ),
    )(data, response, pixel_ids.reshape(1, pixels), shift_bins, shift_bins)


def solution(mesh):
    placed = (P(("groups", "strip"), None, None), P(), P(), P())
    return jax.shard_map(
        on_device,
        mesh=mesh,
        in_specs=placed,
        out_specs=(
            P("strip", "groups", None),
            P(("groups", "strip"), None),
            P(("groups", "strip"), None),
        ),
        check_vma=False,
    )
```

```python
import functools
import math

import jax
import jax.numpy as jnp
from jax import lax
from jax.experimental import pallas as pl
from jax.experimental.pallas import tpu as pltpu
from jax.sharding import PartitionSpec as P

HALO = 16
LAGS = 4
TAPS = 2 * HALO + 1
WIDE = 2 * LAGS + 1
SUB = 8
MESH = pl.DeviceIdType.MESH


def tap_value(offset, bins):
    u = offset.astype(jnp.float32) - bins.astype(jnp.float32) / 4.0
    angle = jnp.pi * u
    safe = jnp.where(u == 0.0, 1.0, angle)
    sinc = jnp.where(u == 0.0, 1.0, jnp.sin(safe) / safe)
    value = sinc * (0.5 + 0.5 * jnp.cos(angle / (HALO + 1)))
    inside = (jnp.abs(u) < HALO + 1) & (jnp.abs(offset) <= HALO)
    return jnp.where(inside, value, 0.0).astype(jnp.bfloat16)


def kernel(
    n, chunks, scaling,
    data_hbm, resp_hbm, ids_hbm, bins_hbm,
    aligned_hbm, sum_hbm, corr_hbm,
    aligned_ref, sum_ref, corr_out_ref, data_ref, resp_ref, ids_ref, bins_ref, bins_smem,
    spread, natural, corrected, received, row_bands, col_bands, row_bins, col_bins,
    row_lines, col_lines, row_taps, col_taps,
    totals, halo_out, halo_in, image, image_pad, image_t, diagonals,
    send_sems, recv_sems, halo_send, halo_recv, image_send, image_recv, own_sem, load_sems, store_sems,
):
    rows, cols, pixels = data_ref.shape
    half_rows = rows // 2
    part = pixels // n
    size = part // chunks
    height = n * rows
    block = min(128, height)
    reach = rows + 2 * HALO
    span = TAPS + (-TAPS) % SUB
    me = lax.axis_index("strip")

    loads = [
        pltpu.make_async_copy(source, target, load_sems.at[k])
        for k, (source, target) in enumerate(
            (
                (resp_hbm, resp_ref),
                (ids_hbm, ids_ref),
                (data_hbm, data_ref),
                (bins_hbm, bins_ref),
                (bins_hbm, bins_smem),
            )
        )
    ]
    for load in loads:
        load.start()

    barrier = pltpu.get_barrier_semaphore()

    def greet(t, carry):
        other = lax.rem(me + t, n)
        pl.semaphore_signal(barrier, inc=1, device_id={"strip": other}, device_id_type=MESH)
        return carry

    lax.fori_loop(1, n, greet, 0)

    loads[0].wait()
    loads[1].wait()
    pick = lax.broadcasted_iota(jnp.int32, (pixels, pixels), 0) == ids_ref[...]
    chosen = jnp.dot(
        resp_ref[...], pick.astype(jnp.float32).astype(jnp.bfloat16), preferred_element_type=jnp.float32
    )
    chosen_t = chosen.T.astype(jnp.bfloat16)
    loads[2].wait()
    for y in range(half_rows):
        both_rows = jnp.concatenate([data_ref[y], data_ref[y + half_rows]], axis=0)
        pair_rows = lax.dot_general(
            chosen_t, both_rows, (((1,), (1,)), ((), ())), preferred_element_type=jnp.float32
        )
        natural[y] = pair_rows.astype(jnp.bfloat16)
        spread[pl.ds(y, pixels, stride=rows), :] = pair_rows[:, :cols]
        spread[pl.ds(y + half_rows, pixels, stride=rows), :] = pair_rows[:, cols:]
    corrected[...] = spread[...].reshape(pixels, rows, cols).astype(jnp.bfloat16)

    pl.semaphore_wait(barrier, n - 1)

    def strip_copy(chunk, other, owner, sender):
        return pltpu.make_async_remote_copy(
            src_ref=corrected.at[pl.ds(owner * part + chunk * size, size)],
            dst_ref=received.at[
                pl.ds(chunk * size, size), pl.ds(pl.multiple_of(HALO + sender * rows, HALO), rows)
            ],
            send_sem=send_sems.at[chunk, other],
            recv_sem=recv_sems.at[chunk, sender],
            device_id={"strip": other},
            device_id_type=MESH,
        )

    def partner(step):
        half = lax.div(step + 1, 2)
        far = n // 2 + jnp.where(lax.rem(step, 2) == 0, half, -half)
        return lax.rem(me + far, n)

    def send_chunk(chunk):
        def one(step, carry):
            other = partner(step)
            strip_copy(chunk, other, other, me).start()
            return carry

        lax.fori_loop(0, n - 1, one, 0)

    for chunk in range(chunks):
        send_chunk(chunk)
    own_copy = pltpu.make_async_copy(
        corrected.at[pl.ds(me * part, part)],
        received.at[:, pl.ds(pl.multiple_of(HALO + me * rows, HALO), rows)],
        own_sem,
    )
    own_copy.start()

    loads[3].wait()
    loads[4].wait()
    taps_at = lax.broadcasted_iota(jnp.int32, (span, pixels), 0) - HALO
    row_taps[...] = tap_value(taps_at, bins_ref[0:1, :]).astype(jnp.float32)
    col_taps[...] = tap_value(taps_at, bins_ref[1:2, :]).astype(jnp.float32)
    totals[...] = jnp.zeros_like(totals)
    outer = row_taps[...].reshape(1, span, pixels) * col_taps[pl.ds(0, TAPS), :].reshape(TAPS, 1, pixels)
    outer = outer.reshape(TAPS * span, pixels).astype(jnp.bfloat16)
    gap = jnp.zeros((TAPS, half_rows, cols), jnp.float32)
    for y in range(half_rows):
        terms = jnp.dot(outer, natural[y], preferred_element_type=jnp.float32)
        terms = terms.reshape(TAPS, span, 2 * cols)
        terms = jnp.concatenate([terms[:, :, :cols], gap], axis=1) + jnp.concatenate(
            [gap, terms[:, :, cols:]], axis=1
        )
        totals[:, pl.ds(y, span + half_rows), :] += terms
    lane = lax.broadcasted_iota(jnp.int32, (reach, cols), 1)
    share = jnp.zeros((reach, cols), jnp.float32)
    for j in range(TAPS):
        shift = j - HALO
        moved = totals[j, pl.ds(0, reach), :]
        if shift:
            moved = pltpu.roll(moved, shift % cols, 1)
            source = lane - shift
            moved = jnp.where((source >= 0) & (source < cols), moved, 0.0)
        share = share + moved
    halo_out[...] = share

    before, after = lax.rem(me + n - 1, n), lax.rem(me + 1, n)

    def halo_copy(side, other, start):
        return pltpu.make_async_remote_copy(
            src_ref=halo_out.at[pl.ds(start, HALO)],
            dst_ref=halo_in.at[side],
            send_sem=halo_send.at[side],
            recv_sem=halo_recv.at[side],
            device_id={"strip": other},
            device_id_type=MESH,
        )

    to_after = halo_copy(0, after, HALO + rows)
    to_before = halo_copy(1, before, 0)
    to_after.start()
    to_before.start()
    for i in range(part):
        row_bins[pl.ds(i, 1), :] = jnp.full((1, 2 * block), bins_smem[0, me * part + i], jnp.int32)
        col_bins[pl.ds(i, 1), :] = jnp.full((1, cols), bins_smem[1, me * part + i], jnp.int32)
    band_lane = lax.broadcasted_iota(jnp.int32, (part, 2 * block), 1)
    col_lane = lax.broadcasted_iota(jnp.int32, (part, cols), 1)
    col_offset = jnp.where(col_lane < cols // 2, col_lane, col_lane - cols)
    row_lines[...] = tap_value(HALO - band_lane, row_bins[...]).astype(jnp.float32)
    col_lines[...] = tap_value(col_offset, col_bins[...]).astype(jnp.float32)
    square = (cols, cols)
    near = (
        jnp.abs(lax.broadcasted_iota(jnp.int32, square, 0) - lax.broadcasted_iota(jnp.int32, square, 1))
        <= HALO
    )

    def bands(i, carry):
        row_band = jnp.broadcast_to(row_lines[pl.ds(i, 1), :], (block, 2 * block))
        row_bands[i] = pltpu.roll(row_band, 0, 1, stride=1, stride_axis=0).astype(jnp.bfloat16)
        col_band = jnp.broadcast_to(col_lines[pl.ds(i, 1), :], square)
        col_band = pltpu.roll(col_band, 0, 1, stride=1, stride_axis=0)
        col_bands[i] = jnp.where(near, col_band, 0.0).astype(jnp.bfloat16)
        return carry

    lax.fori_loop(0, part, bands, 0)
    edge = jnp.zeros((part, HALO, cols), jnp.bfloat16)
    received[:, pl.ds(0, HALO), :] = edge
    received[:, pl.ds(HALO + height, HALO), :] = edge

    to_after.wait_recv()
    to_before.wait_recv()
    mine = halo_out[pl.ds(HALO, rows), :]
    fill = jnp.zeros((rows - HALO, cols), jnp.float32)
    from_before = jnp.where(me > 0, halo_in[0], 0.0)
    from_after = jnp.where(me < n - 1, halo_in[1], 0.0)
    if rows > HALO:
        from_before = jnp.concatenate([from_before, fill], axis=0)
        from_after = jnp.concatenate([fill, from_after], axis=0)
    mine = mine + from_before + from_after
    sum_ref[...] = mine
    sum_store = pltpu.make_async_copy(sum_ref, sum_hbm, store_sems.at[chunks])
    sum_store.start()
    image[pl.ds(pl.multiple_of(me * rows, HALO), rows), :] = mine.astype(jnp.bfloat16)

    def image_copy(other, sender):
        place = pl.ds(pl.multiple_of(sender * rows, HALO), rows)
        return pltpu.make_async_remote_copy(
            src_ref=image.at[place],
            dst_ref=image.at[place],
            send_sem=image_send.at[other],
            recv_sem=image_recv.at[sender],
            device_id={"strip": other},
            device_id_type=MESH,
        )

    def send_image(step, carry):
        image_copy(partner(step), me).start()
        return carry

    lax.fori_loop(0, n - 1, send_image, 0)

    def aligned_store(chunk):
        place = pl.ds(chunk * size, size)
        return pltpu.make_async_copy(aligned_ref.at[place], aligned_hbm.at[place], store_sems.at[chunk])

    def align(chunk):
        def await_strip(step, inner):
            other = lax.rem(me + step, n)
            strip_copy(chunk, other, other, other).wait_recv()
            return inner

        lax.fori_loop(1, n, await_strip, 0)

        def one(index, inner):
            i = chunk * size + index
            row_band = row_bands[i][:, : block + 2 * HALO]
            col_band = col_bands[i]
            for start in range(0, height, block):
                window = received[i, pl.ds(start, block + 2 * HALO), :]
                moved = jnp.dot(row_band, window, preferred_element_type=jnp.float32)
                moved = jnp.dot(
                    moved.astype(jnp.bfloat16), col_band, preferred_element_type=jnp.float32
                )
                aligned_ref[i, pl.ds(start, block), :] = moved.astype(jnp.bfloat16)
            return inner

        lax.fori_loop(0, size, one, 0, unroll=True)
        aligned_store(chunk).start()

    own_copy.wait()
    align(0)

    def await_image(step, carry):
        other = lax.rem(me + step, n)
        image_copy(other, other).wait_recv()
        return carry

    lax.fori_loop(1, n, await_image, 0)
    image_pad[pl.ds(0, SUB), :] = jnp.zeros((SUB, cols), jnp.float32)
    image_pad[pl.ds(SUB + height, SUB), :] = jnp.zeros((SUB, cols), jnp.float32)
    image_pad[pl.ds(SUB, height), :] = image[...].astype(jnp.float32)
    for a in range(WIDE):
        window = image_pad[pl.ds(SUB + a - LAGS, height), :]
        image_t[pl.ds(a * cols, cols), :] = window.T.astype(jnp.bfloat16)

    low_lane = lax.broadcasted_iota(jnp.int32, (SUB, cols), 1) < cols // 2
    tail_lane = lax.broadcasted_iota(jnp.int32, (SUB, cols), 1)
    tail_keep = (tail_lane < SUB) | (tail_lane >= cols // 2)
    pieces = cols // SUB

    def correlate(chunk):
        def pair(index, inner):
            first = chunk * size + 2 * index
            both = jnp.concatenate([aligned_ref[first], aligned_ref[first + 1]], axis=1)
            for a in range(WIDE):
                products = jnp.dot(
                    image_t[pl.ds(a * cols, cols), :], both, preferred_element_type=jnp.float32
                )
                for k in range(2):
                    total = None
                    for piece in range(pieces):
                        term = products[piece * SUB : (piece + 1) * SUB, k * cols : (k + 1) * cols]
                        if piece:
                            term = pltpu.roll(term, cols - piece * SUB, 1)
                        if piece == 0:
                            term = jnp.where(low_lane, term, 0.0)
                        elif piece == pieces - 1:
                            term = jnp.where(tail_keep, term, 0.0)
                        total = term if total is None else total + term
                    place = pl.multiple_of((a * part + first + k) * SUB, SUB)
                    diagonals[pl.ds(place, SUB), :] = total
            return inner

        lax.fori_loop(0, size // 2, pair, 0)

    correlate(0)

    def work_chunk(chunk, carry):
        align(chunk)
        correlate(chunk)
        return carry

    lax.fori_loop(1, chunks, work_chunk, 0)

    gathered = jnp.zeros((WIDE * part, cols), jnp.float32)
    lane_in = lax.broadcasted_iota(jnp.int32, square, 0)
    lane_out = lax.broadcasted_iota(jnp.int32, square, 1)
    for s in range(SUB):
        wanted = s - (lane_out - LAGS)
        wanted = jnp.where(wanted < 0, wanted + cols, wanted)
        choose = ((lane_in == wanted) & (lane_out < WIDE)).astype(jnp.float32)
        gathered = gathered + jnp.dot(
            diagonals[pl.ds(s, WIDE * part, stride=SUB), :],
            choose,
            precision=lax.Precision.HIGHEST,
            preferred_element_type=jnp.float32,
        )
    result = jnp.zeros((part, cols), jnp.float32)
    for a in range(WIDE):
        lags = gathered[a * part : (a + 1) * part, :]
        result = result + (pltpu.roll(lags, a * WIDE, 1) if a else lags)
    corr_out_ref[...] = (result * scaling)[:, : WIDE * WIDE]
    corr_store = pltpu.make_async_copy(corr_out_ref, corr_hbm, store_sems.at[chunks + 1])
    corr_store.start()

    def drain(step, carry):
        other = lax.rem(me + step, n)
        for chunk in range(chunks):
            strip_copy(chunk, other, other, me).wait_send()
        image_copy(other, me).wait_send()
        return carry

    lax.fori_loop(1, n, drain, 0)
    to_after.wait_send()
    to_before.wait_send()
    for chunk in range(chunks):
        aligned_store(chunk).wait()
    sum_store.wait()
    corr_store.wait()


def write_out(*refs):
    copies = [pltpu.make_async_copy(refs[k], refs[3 + k], refs[6].at[k]) for k in range(3)]
    for copy in copies:
        copy.start()
    for copy in copies:
        copy.wait()


def on_device(data, response, pixel_ids, shift_bins):
    rows, cols, pixels = data.shape
    n = lax.axis_size("strip")
    part = pixels // n
    chunks = max(1, part // 4)
    height = n * rows
    block = min(128, height)
    reach = rows + 2 * HALO
    assert rows >= HALO and rows % 16 == 0 and (part // chunks) % 2 == 0 and height % block == 0
    scaling = 1.0 / math.sqrt(pixels * height * cols)
    span = TAPS + (-TAPS) % SUB
    hbm = pl.BlockSpec(memory_space=pltpu.HBM)
    bf16, f32 = jnp.bfloat16, jnp.float32
    shapes = (
        jax.ShapeDtypeStruct((part, height, cols), bf16),
        jax.ShapeDtypeStruct((rows, cols), f32),
        jax.ShapeDtypeStruct((part, WIDE * WIDE), f32),
    )
    results = pl.pallas_call(
        functools.partial(kernel, n, chunks, scaling),
        out_shape=shapes,
        in_specs=[hbm] * 4,
        out_specs=(hbm, hbm, hbm),
        scratch_shapes=[
            pltpu.VMEM((part, height, cols), bf16),
            pltpu.VMEM((rows, cols), f32),
            pltpu.VMEM((part, WIDE * WIDE), f32),
            pltpu.VMEM((rows, cols, pixels), bf16),
            pltpu.VMEM((pixels, pixels), bf16),
            pltpu.VMEM((1, pixels), jnp.int32),
            pltpu.VMEM((2, pixels), jnp.int32),
            pltpu.SMEM((2, pixels), jnp.int32),
            pltpu.VMEM((pixels * rows, cols), f32),
            pltpu.VMEM((rows // 2, pixels, 2 * cols), bf16),
            pltpu.VMEM((pixels, rows, cols), bf16),
            pltpu.VMEM((part, height + 2 * HALO, cols), bf16),
            pltpu.VMEM((part, block, 2 * block), bf16),
            pltpu.VMEM((part, cols, cols), bf16),
            pltpu.VMEM((part, 2 * block), jnp.int32),
            pltpu.VMEM((part, cols), jnp.int32),
            pltpu.VMEM((part, 2 * block), f32),
            pltpu.VMEM((part, cols), f32),
            pltpu.VMEM((span, pixels), f32),
            pltpu.VMEM((span, pixels), f32),
            pltpu.VMEM((TAPS, span + rows, cols), f32),
            pltpu.VMEM((reach, cols), f32),
            pltpu.VMEM((2, HALO, cols), f32),
            pltpu.VMEM((height, cols), bf16),
            pltpu.VMEM((height + 2 * SUB, cols), f32),
            pltpu.VMEM((WIDE * cols, height), bf16),
            pltpu.VMEM((WIDE * part * SUB, cols), f32),
            pltpu.SemaphoreType.DMA((chunks, n)),
            pltpu.SemaphoreType.DMA((chunks, n)),
            pltpu.SemaphoreType.DMA((2,)),
            pltpu.SemaphoreType.DMA((2,)),
            pltpu.SemaphoreType.DMA((n,)),
            pltpu.SemaphoreType.DMA((n,)),
            pltpu.SemaphoreType.DMA(()),
            pltpu.SemaphoreType.DMA((5,)),
            pltpu.SemaphoreType.DMA((chunks + 2,)),
        ],
        compiler_params=pltpu.CompilerParams(
            collective_id=0, has_side_effects=True, vmem_limit_bytes=56 * 1024 * 1024
        ),
    )(data, response, pixel_ids.reshape(1, pixels), shift_bins)
    return pl.pallas_call(
        write_out,
        out_shape=shapes,
        in_specs=[hbm] * 3,
        out_specs=(hbm, hbm, hbm),
        scratch_shapes=[pltpu.SemaphoreType.DMA((3,))],
        compiler_params=pltpu.CompilerParams(vmem_limit_bytes=56 * 1024 * 1024),
    )(*results)


def solution(mesh):
    placed = (P(("groups", "strip"), None, None), P(), P(), P())
    return jax.shard_map(
        on_device,
        mesh=mesh,
        in_specs=placed,
        out_specs=(
            P("strip", "groups", None),
            P(("groups", "strip"), None),
            P(("groups", "strip"), None),
        ),
        check_vma=False,
    )
```

```python
import functools
import math

import jax
import jax.numpy as jnp
from jax import lax
from jax.experimental import pallas as pl
from jax.experimental.pallas import tpu as pltpu
from jax.sharding import PartitionSpec as P

HALO = 16
LAGS = 4
TAPS = 2 * HALO + 1
WIDE = 2 * LAGS + 1
SUB = 8
MESH = pl.DeviceIdType.MESH


def tap_value(offset, bins):
    u = offset.astype(jnp.float32) - bins.astype(jnp.float32) / 4.0
    angle = jnp.pi * u
    safe = jnp.where(u == 0.0, 1.0, angle)
    sinc = jnp.where(u == 0.0, 1.0, jnp.sin(safe) / safe)
    value = sinc * (0.5 + 0.5 * jnp.cos(angle / (HALO + 1)))
    inside = (jnp.abs(u) < HALO + 1) & (jnp.abs(offset) <= HALO)
    return jnp.where(inside, value, 0.0).astype(jnp.bfloat16)


def kernel(
    n, chunks, scaling,
    data_hbm, resp_hbm, ids_hbm, bins_hbm,
    aligned_ref, sum_ref, corr_out_ref,
    data_ref, resp_ref, ids_ref, bins_ref, bins_smem,
    spread, natural, corrected, received, row_bands, col_bands, row_bins, col_bins,
    row_lines, col_lines, row_taps, col_taps,
    totals, halo_out, halo_in, image, image_pad, image_t, diagonals,
    send_sems, recv_sems, halo_send, halo_recv, image_send, image_recv, own_sem, load_sems,
):
    rows, cols, pixels = data_ref.shape
    half_rows = rows // 2
    part = pixels // n
    size = part // chunks
    height = n * rows
    block = min(128, height)
    reach = rows + 2 * HALO
    span = TAPS + (-TAPS) % SUB
    me = lax.axis_index("strip")

    loads = [
        pltpu.make_async_copy(source, target, load_sems.at[k])
        for k, (source, target) in enumerate(
            (
                (resp_hbm, resp_ref),
                (ids_hbm, ids_ref),
                (data_hbm, data_ref),
                (bins_hbm, bins_ref),
                (bins_hbm, bins_smem),
            )
        )
    ]
    for load in loads:
        load.start()

    barrier = pltpu.get_barrier_semaphore()

    def greet(t, carry):
        other = lax.rem(me + t, n)
        pl.semaphore_signal(barrier, inc=1, device_id={"strip": other}, device_id_type=MESH)
        return carry

    lax.fori_loop(1, n, greet, 0)

    loads[0].wait()
    loads[1].wait()
    pick = lax.broadcasted_iota(jnp.int32, (pixels, pixels), 0) == ids_ref[...]
    chosen = jnp.dot(
        resp_ref[...], pick.astype(jnp.float32).astype(jnp.bfloat16), preferred_element_type=jnp.float32
    )
    chosen_t = chosen.T.astype(jnp.bfloat16)
    loads[2].wait()
    for y in range(half_rows):
        both_rows = jnp.concatenate([data_ref[y], data_ref[y + half_rows]], axis=0)
        pair_rows = lax.dot_general(
            chosen_t, both_rows, (((1,), (1,)), ((), ())), preferred_element_type=jnp.float32
        )
        natural[y] = pair_rows.astype(jnp.bfloat16)
        spread[pl.ds(y, pixels, stride=rows), :] = pair_rows[:, :cols]
        spread[pl.ds(y + half_rows, pixels, stride=rows), :] = pair_rows[:, cols:]
    corrected[...] = spread[...].reshape(pixels, rows, cols).astype(jnp.bfloat16)

    pl.semaphore_wait(barrier, n - 1)

    def strip_copy(chunk, other, owner, sender):
        return pltpu.make_async_remote_copy(
            src_ref=corrected.at[pl.ds(owner * part + chunk * size, size)],
            dst_ref=received.at[chunk, sender + 1],
            send_sem=send_sems.at[chunk, other],
            recv_sem=recv_sems.at[chunk, sender],
            device_id={"strip": other},
            device_id_type=MESH,
        )

    def partner(step):
        half = lax.div(step + 1, 2)
        even = lax.rem(step, 2) == 0
        if n & (n - 1):
            return lax.rem(me + n // 2 + jnp.where(even, half, -half), n)
        return me ^ jnp.where(even, n // 2 + half, half)

    def send_chunk(chunk):
        def one(step, carry):
            other = partner(step)
            strip_copy(chunk, other, other, me).start()
            return carry

        lax.fori_loop(0, n - 1, one, 0)

    def await_left(chunk):
        def one(step, carry):
            other = partner(step)
            strip_copy(chunk, other, other, me).wait_send()
            return carry

        lax.fori_loop(0, n - 1, one, 0)

    ahead = min(2, chunks)
    for chunk in range(ahead):
        send_chunk(chunk)
    own_copies = [
        pltpu.make_async_copy(
            corrected.at[pl.ds(me * part + chunk * size, size)],
            received.at[chunk, me + 1],
            own_sem.at[chunk],
        )
        for chunk in range(chunks)
    ]
    for own_copy in own_copies:
        own_copy.start()

    loads[3].wait()
    loads[4].wait()
    taps_at = lax.broadcasted_iota(jnp.int32, (span, pixels), 0) - HALO
    row_taps[...] = tap_value(taps_at, bins_ref[0:1, :]).astype(jnp.float32)
    col_taps[...] = tap_value(taps_at, bins_ref[1:2, :]).astype(jnp.float32)
    totals[...] = jnp.zeros_like(totals)
    outer = row_taps[...].reshape(1, span, pixels) * col_taps[pl.ds(0, TAPS), :].reshape(TAPS, 1, pixels)
    outer = outer.reshape(TAPS * span, pixels).astype(jnp.bfloat16)
    gap = jnp.zeros((TAPS, half_rows, cols), jnp.float32)
    for y in range(half_rows):
        terms = jnp.dot(outer, natural[y], preferred_element_type=jnp.float32)
        terms = terms.reshape(TAPS, span, 2 * cols)
        terms = jnp.concatenate([terms[:, :, :cols], gap], axis=1) + jnp.concatenate(
            [gap, terms[:, :, cols:]], axis=1
        )
        totals[:, pl.ds(y, span + half_rows), :] += terms
    lane = lax.broadcasted_iota(jnp.int32, (reach, cols), 1)
    share = jnp.zeros((reach, cols), jnp.float32)
    for j in range(TAPS):
        shift = j - HALO
        moved = totals[j, pl.ds(0, reach), :]
        if shift:
            moved = pltpu.roll(moved, shift % cols, 1)
            source = lane - shift
            moved = jnp.where((source >= 0) & (source < cols), moved, 0.0)
        share = share + moved
    halo_out[...] = share

    before, after = lax.rem(me + n - 1, n), lax.rem(me + 1, n)

    def halo_copy(side, other, start):
        return pltpu.make_async_remote_copy(
            src_ref=halo_out.at[pl.ds(start, HALO)],
            dst_ref=halo_in.at[side],
            send_sem=halo_send.at[side],
            recv_sem=halo_recv.at[side],
            device_id={"strip": other},
            device_id_type=MESH,
        )

    to_after = halo_copy(0, after, HALO + rows)
    to_before = halo_copy(1, before, 0)
    to_after.start()
    to_before.start()
    for i in range(part):
        row_bins[pl.ds(i, 1), :] = jnp.full((1, 2 * block), bins_smem[0, me * part + i], jnp.int32)
        col_bins[pl.ds(i, 1), :] = jnp.full((1, cols), bins_smem[1, me * part + i], jnp.int32)
    band_lane = lax.broadcasted_iota(jnp.int32, (part, 2 * block), 1)
    col_lane = lax.broadcasted_iota(jnp.int32, (part, cols), 1)
    col_offset = jnp.where(col_lane < cols // 2, col_lane, col_lane - cols)
    row_lines[...] = tap_value(HALO - band_lane, row_bins[...]).astype(jnp.float32)
    col_lines[...] = tap_value(col_offset, col_bins[...]).astype(jnp.float32)
    square = (cols, cols)
    near = (
        jnp.abs(lax.broadcasted_iota(jnp.int32, square, 0) - lax.broadcasted_iota(jnp.int32, square, 1))
        <= HALO
    )

    def bands(i, carry):
        row_band = jnp.broadcast_to(row_lines[pl.ds(i, 1), :], (block, 2 * block))
        row_bands[i] = pltpu.roll(row_band, 0, 1, stride=1, stride_axis=0).astype(jnp.bfloat16)
        col_band = jnp.broadcast_to(col_lines[pl.ds(i, 1), :], square)
        col_band = pltpu.roll(col_band, 0, 1, stride=1, stride_axis=0)
        col_bands[i] = jnp.where(near, col_band, 0.0).astype(jnp.bfloat16)
        return carry

    lax.fori_loop(0, part, bands, 0)
    edge = jnp.zeros((chunks, size, rows, cols), jnp.bfloat16)
    received[:, 0] = edge
    received[:, n + 1] = edge
    if chunks > 2:
        await_left(0)
        send_chunk(2)

    to_after.wait_recv()
    to_before.wait_recv()
    mine = halo_out[pl.ds(HALO, rows), :]
    fill = jnp.zeros((rows - HALO, cols), jnp.float32)
    from_before = jnp.where(me > 0, halo_in[0], 0.0)
    from_after = jnp.where(me < n - 1, halo_in[1], 0.0)
    if rows > HALO:
        from_before = jnp.concatenate([from_before, fill], axis=0)
        from_after = jnp.concatenate([fill, from_after], axis=0)
    mine = mine + from_before + from_after
    sum_ref[...] = mine
    image[pl.ds(pl.multiple_of(me * rows, HALO), rows), :] = mine.astype(jnp.bfloat16)

    def image_copy(other, sender):
        place = pl.ds(pl.multiple_of(sender * rows, HALO), rows)
        return pltpu.make_async_remote_copy(
            src_ref=image.at[place],
            dst_ref=image.at[place],
            send_sem=image_send.at[other],
            recv_sem=image_recv.at[sender],
            device_id={"strip": other},
            device_id_type=MESH,
        )

    def send_image(step, carry):
        image_copy(partner(step), me).start()
        return carry

    lax.fori_loop(0, n - 1, send_image, 0)

    def align(chunk):
        def await_strip(step, inner):
            other = lax.rem(me + step, n)
            strip_copy(chunk, other, other, other).wait_recv()
            return inner

        lax.fori_loop(1, n, await_strip, 0)

        def one(index, inner):
            i = chunk * size + index
            row_band = row_bands[i][:, : block + 2 * HALO]
            col_band = col_bands[i]
            for start in range(0, height, block):
                window = received[chunk, pl.ds(start // rows, block // rows + 2), index]
                window = window.reshape(block + 2 * rows, cols)[rows - HALO : rows + block + HALO]
                moved = jnp.dot(row_band, window, preferred_element_type=jnp.float32)
                moved = jnp.dot(
                    moved.astype(jnp.bfloat16), col_band, preferred_element_type=jnp.float32
                )
                aligned_ref[i, pl.ds(start, block), :] = moved.astype(jnp.bfloat16)
            return inner

        lax.fori_loop(0, size, one, 0, unroll=True)

    for own_copy in own_copies:
        own_copy.wait()
    align(0)

    def await_image(step, carry):
        other = lax.rem(me + step, n)
        image_copy(other, other).wait_recv()
        return carry

    lax.fori_loop(1, n, await_image, 0)
    image_pad[pl.ds(0, SUB), :] = jnp.zeros((SUB, cols), jnp.float32)
    image_pad[pl.ds(SUB + height, SUB), :] = jnp.zeros((SUB, cols), jnp.float32)
    image_pad[pl.ds(SUB, height), :] = image[...].astype(jnp.float32)
    for a in range(WIDE):
        window = image_pad[pl.ds(SUB + a - LAGS, height), :]
        image_t[pl.ds(a * cols, cols), :] = window.T.astype(jnp.bfloat16)

    for chunk in range(3, chunks):
        await_left(chunk - 2)
        send_chunk(chunk)
    low_lane = lax.broadcasted_iota(jnp.int32, (SUB, cols), 1) < cols // 2
    tail_lane = lax.broadcasted_iota(jnp.int32, (SUB, cols), 1)
    tail_keep = (tail_lane < SUB) | (tail_lane >= cols // 2)
    pieces = cols // SUB

    def correlate(chunk):
        def pair(index, inner):
            first = chunk * size + 2 * index
            both = jnp.concatenate([aligned_ref[first], aligned_ref[first + 1]], axis=1)
            for a in range(WIDE):
                products = jnp.dot(
                    image_t[pl.ds(a * cols, cols), :], both, preferred_element_type=jnp.float32
                )
                for k in range(2):
                    total = None
                    for piece in range(pieces):
                        term = products[piece * SUB : (piece + 1) * SUB, k * cols : (k + 1) * cols]
                        if piece:
                            term = pltpu.roll(term, cols - piece * SUB, 1)
                        if piece == 0:
                            term = jnp.where(low_lane, term, 0.0)
                        elif piece == pieces - 1:
                            term = jnp.where(tail_keep, term, 0.0)
                        total = term if total is None else total + term
                    place = pl.multiple_of((a * part + first + k) * SUB, SUB)
                    diagonals[pl.ds(place, SUB), :] = total
            return inner

        lax.fori_loop(0, size // 2, pair, 0)

    correlate(0)

    def work_chunk(chunk, carry):
        align(chunk)
        correlate(chunk)
        return carry

    lax.fori_loop(1, chunks, work_chunk, 0)

    gathered = jnp.zeros((WIDE * part, cols), jnp.float32)
    for s in range(SUB):
        lines = diagonals[pl.ds(s, WIDE * part, stride=SUB), :]
        turn = (LAGS - s) % cols
        gathered = gathered + (pltpu.roll(lines, turn, 1) if turn else lines)
    lane_in = lax.broadcasted_iota(jnp.int32, square, 0)
    lane_out = lax.broadcasted_iota(jnp.int32, square, 1)
    mirror = ((lane_in + lane_out == 2 * LAGS) & (lane_out < WIDE)).astype(jnp.float32)
    gathered = jnp.dot(
        gathered, mirror, precision=lax.Precision.HIGHEST, preferred_element_type=jnp.float32
    )
    result = jnp.zeros((part, cols), jnp.float32)
    for a in range(WIDE):
        lags = gathered[a * part : (a + 1) * part, :]
        result = result + (pltpu.roll(lags, a * WIDE, 1) if a else lags)
    corr_out_ref[...] = (result * scaling)[:, : WIDE * WIDE]

    def drain(step, carry):
        image_copy(lax.rem(me + step, n), me).wait_send()
        return carry

    lax.fori_loop(1, n, drain, 0)
    for chunk in range(max(0, chunks - 2), chunks):
        await_left(chunk)
    to_after.wait_send()
    to_before.wait_send()


def write_out(*refs):
    copies = [pltpu.make_async_copy(refs[k], refs[3 + k], refs[6].at[k]) for k in range(3)]
    for copy in copies:
        copy.start()
    for copy in copies:
        copy.wait()


def on_device(data, response, pixel_ids, shift_bins):
    rows, cols, pixels = data.shape
    n = lax.axis_size("strip")
    part = pixels // n
    chunks = max(1, part // 4)
    height = n * rows
    block = min(128, height)
    reach = rows + 2 * HALO
    assert rows >= HALO and rows % 16 == 0 and block % rows == 0 and (part // chunks) % 2 == 0 and height % block == 0
    scaling = 1.0 / math.sqrt(pixels * height * cols)
    span = TAPS + (-TAPS) % SUB
    vmem = pl.BlockSpec(memory_space=pltpu.VMEM)
    hbm = pl.BlockSpec(memory_space=pltpu.HBM)
    bf16, f32 = jnp.bfloat16, jnp.float32
    shapes = (
        jax.ShapeDtypeStruct((part, height, cols), bf16),
        jax.ShapeDtypeStruct((rows, cols), f32),
        jax.ShapeDtypeStruct((part, WIDE * WIDE), f32),
    )
    results = pl.pallas_call(
        functools.partial(kernel, n, chunks, scaling),
        out_shape=shapes,
        in_specs=[hbm] * 4,
        out_specs=(vmem, vmem, vmem),
        scratch_shapes=[
            pltpu.VMEM((rows, cols, pixels), bf16),
            pltpu.VMEM((pixels, pixels), bf16),
            pltpu.VMEM((1, pixels), jnp.int32),
            pltpu.VMEM((2, pixels), jnp.int32),
            pltpu.SMEM((2, pixels), jnp.int32),
            pltpu.VMEM((pixels * rows, cols), f32),
            pltpu.VMEM((rows // 2, pixels, 2 * cols), bf16),
            pltpu.VMEM((pixels, rows, cols), bf16),
            pltpu.VMEM((chunks, n + 2, part // chunks, rows, cols), bf16),
            pltpu.VMEM((part, block, 2 * block), bf16),
            pltpu.VMEM((part, cols, cols), bf16),
            pltpu.VMEM((part, 2 * block), jnp.int32),
            pltpu.VMEM((part, cols), jnp.int32),
            pltpu.VMEM((part, 2 * block), f32),
            pltpu.VMEM((part, cols), f32),
            pltpu.VMEM((span, pixels), f32),
            pltpu.VMEM((span, pixels), f32),
            pltpu.VMEM((TAPS, span + rows, cols), f32),
            pltpu.VMEM((reach, cols), f32),
            pltpu.VMEM((2, HALO, cols), f32),
            pltpu.VMEM((height, cols), bf16),
            pltpu.VMEM((height + 2 * SUB, cols), f32),
            pltpu.VMEM((WIDE * cols, height), bf16),
            pltpu.VMEM((WIDE * part * SUB, cols), f32),
            pltpu.SemaphoreType.DMA((chunks, n)),
            pltpu.SemaphoreType.DMA((chunks, n)),
            pltpu.SemaphoreType.DMA((2,)),
            pltpu.SemaphoreType.DMA((2,)),
            pltpu.SemaphoreType.DMA((n,)),
            pltpu.SemaphoreType.DMA((n,)),
            pltpu.SemaphoreType.DMA((chunks,)),
            pltpu.SemaphoreType.DMA((5,)),
        ],
        compiler_params=pltpu.CompilerParams(
            collective_id=0, has_side_effects=True, vmem_limit_bytes=48 * 1024 * 1024
        ),
    )(*(pltpu.with_memory_space_constraint(a, pltpu.HBM) for a in (data, response, pixel_ids.reshape(1, pixels), shift_bins)))
    return pl.pallas_call(
        write_out,
        out_shape=shapes,
        in_specs=[vmem] * 3,
        out_specs=(hbm, hbm, hbm),
        scratch_shapes=[pltpu.SemaphoreType.DMA((3,))],
    )(*results)


def solution(mesh):
    placed = (P(("groups", "strip"), None, None), P(), P(), P())
    return jax.shard_map(
        on_device,
        mesh=mesh,
        in_specs=placed,
        out_specs=(
            P("strip", "groups", None),
            P(("groups", "strip"), None),
            P(("groups", "strip"), None),
        ),
        check_vma=False,
    )
```

```python
import functools
import math

import jax
import jax.numpy as jnp
from jax import lax
from jax.experimental import pallas as pl
from jax.experimental.pallas import tpu as pltpu
from jax.sharding import PartitionSpec as P

HALO = 16
LAGS = 4
TAPS = 2 * HALO + 1
WIDE = 2 * LAGS + 1
SUB = 8
MESH = pl.DeviceIdType.MESH


def tap_value(offset, bins):
    u = offset.astype(jnp.float32) - bins.astype(jnp.float32) / 4.0
    angle = jnp.pi * u
    safe = jnp.where(u == 0.0, 1.0, angle)
    sinc = jnp.where(u == 0.0, 1.0, jnp.sin(safe) / safe)
    value = sinc * (0.5 + 0.5 * jnp.cos(angle / (HALO + 1)))
    inside = (jnp.abs(u) < HALO + 1) & (jnp.abs(offset) <= HALO)
    return jnp.where(inside, value, 0.0).astype(jnp.bfloat16)


def kernel(
    n, chunks, scaling,
    data_hbm, resp_hbm, ids_hbm, bins_hbm,
    aligned_ref, sum_ref, corr_out_ref,
    data_ref, resp_ref, ids_ref, bins_ref, bins_smem,
    spread, natural, corrected, received, row_bands, col_bands, row_bins, col_bins,
    row_lines, col_lines, row_taps, col_taps, outer_taps,
    totals, halo_out, halo_in, image, image_pad, image_t, diagonals,
    send_sems, recv_sems, halo_send, halo_recv, image_send, image_recv, own_sem, load_sems,
):
    rows, cols, pixels = data_ref.shape
    half_rows = rows // 2
    part = pixels // n
    size = part // chunks
    height = n * rows
    block = min(128, height)
    reach = rows + 2 * HALO
    span = TAPS + (-TAPS) % SUB
    me = lax.axis_index("strip")

    loads = [
        pltpu.make_async_copy(source, target, load_sems.at[k])
        for k, (source, target) in enumerate(
            (
                (resp_hbm, resp_ref),
                (ids_hbm, ids_ref),
                (data_hbm, data_ref),
                (bins_hbm, bins_ref),
                (bins_hbm, bins_smem),
            )
        )
    ]
    for load in loads:
        load.start()

    barrier = pltpu.get_barrier_semaphore()

    def greet(t, carry):
        other = lax.rem(me + t, n)
        pl.semaphore_signal(barrier, inc=1, device_id={"strip": other}, device_id_type=MESH)
        return carry

    lax.fori_loop(1, n, greet, 0)

    loads[0].wait()
    loads[1].wait()
    pick = lax.broadcasted_iota(jnp.int32, (pixels, pixels), 0) == ids_ref[...]
    chosen = jnp.dot(
        resp_ref[...], pick.astype(jnp.float32).astype(jnp.bfloat16), preferred_element_type=jnp.float32
    )
    chosen_t = chosen.T.astype(jnp.bfloat16)
    loads[3].wait()
    loads[4].wait()
    taps_at = lax.broadcasted_iota(jnp.int32, (span, pixels), 0) - HALO
    row_taps[...] = tap_value(taps_at, bins_ref[0:1, :]).astype(jnp.float32)
    col_taps[...] = tap_value(taps_at, bins_ref[1:2, :]).astype(jnp.float32)
    totals[...] = jnp.zeros_like(totals)
    outer = row_taps[...].reshape(1, span, pixels) * col_taps[pl.ds(0, TAPS), :].reshape(TAPS, 1, pixels)
    outer_taps[...] = outer.reshape(TAPS * span, pixels).astype(jnp.bfloat16)
    loads[2].wait()
    for y in range(half_rows):
        both_rows = jnp.concatenate([data_ref[y], data_ref[y + half_rows]], axis=0)
        pair_rows = lax.dot_general(
            chosen_t, both_rows, (((1,), (1,)), ((), ())), preferred_element_type=jnp.float32
        )
        natural[y] = pair_rows.astype(jnp.bfloat16)
        spread[pl.ds(y, pixels, stride=rows), :] = pair_rows[:, :cols]
        spread[pl.ds(y + half_rows, pixels, stride=rows), :] = pair_rows[:, cols:]
    corrected[...] = spread[...].reshape(pixels, rows, cols).astype(jnp.bfloat16)

    pl.semaphore_wait(barrier, n - 1)

    def strip_copy(chunk, other, owner, sender):
        return pltpu.make_async_remote_copy(
            src_ref=corrected.at[pl.ds(owner * part + chunk * size, size)],
            dst_ref=received.at[chunk, sender + 1],
            send_sem=send_sems.at[chunk, other],
            recv_sem=recv_sems.at[chunk, sender],
            device_id={"strip": other},
            device_id_type=MESH,
        )

    def partner(step):
        half = lax.div(step + 1, 2)
        even = lax.rem(step, 2) == 0
        if n & (n - 1):
            return lax.rem(me + n // 2 + jnp.where(even, half, -half), n)
        return me ^ jnp.where(even, n // 2 + half, half)

    def send_chunk(chunk):
        def one(step, carry):
            other = partner(step)
            strip_copy(chunk, other, other, me).start()
            return carry

        lax.fori_loop(0, n - 1, one, 0)

    def await_left(chunk):
        def one(step, carry):
            other = partner(step)
            strip_copy(chunk, other, other, me).wait_send()
            return carry

        lax.fori_loop(0, n - 1, one, 0)

    send_chunk(0)
    own_copies = [
        pltpu.make_async_copy(
            corrected.at[pl.ds(me * part + chunk * size, size)],
            received.at[chunk, me + 1],
            own_sem.at[chunk],
        )
        for chunk in range(chunks)
    ]
    for own_copy in own_copies:
        own_copy.start()

    gap = jnp.zeros((TAPS, half_rows, cols), jnp.float32)
    for y in range(half_rows):
        terms = jnp.dot(outer_taps[...], natural[y], preferred_element_type=jnp.float32)
        terms = terms.reshape(TAPS, span, 2 * cols)
        terms = jnp.concatenate([terms[:, :, :cols], gap], axis=1) + jnp.concatenate(
            [gap, terms[:, :, cols:]], axis=1
        )
        totals[:, pl.ds(y, span + half_rows), :] += terms
    lane = lax.broadcasted_iota(jnp.int32, (reach, cols), 1)
    share = jnp.zeros((reach, cols), jnp.float32)
    for j in range(TAPS):
        shift = j - HALO
        moved = totals[j, pl.ds(0, reach), :]
        if shift:
            moved = pltpu.roll(moved, shift % cols, 1)
            source = lane - shift
            moved = jnp.where((source >= 0) & (source < cols), moved, 0.0)
        share = share + moved
    halo_out[...] = share

    before, after = lax.rem(me + n - 1, n), lax.rem(me + 1, n)

    def halo_copy(side, other, start):
        return pltpu.make_async_remote_copy(
            src_ref=halo_out.at[pl.ds(start, HALO)],
            dst_ref=halo_in.at[side],
            send_sem=halo_send.at[side],
            recv_sem=halo_recv.at[side],
            device_id={"strip": other},
            device_id_type=MESH,
        )

    to_after = halo_copy(0, after, HALO + rows)
    to_before = halo_copy(1, before, 0)
    to_after.start()
    to_before.start()
    if chunks > 1:
        send_chunk(1)
    for i in range(part):
        row_bins[pl.ds(i, 1), :] = jnp.full((1, 2 * block), bins_smem[0, me * part + i], jnp.int32)
        col_bins[pl.ds(i, 1), :] = jnp.full((1, cols), bins_smem[1, me * part + i], jnp.int32)
    band_lane = lax.broadcasted_iota(jnp.int32, (part, 2 * block), 1)
    col_lane = lax.broadcasted_iota(jnp.int32, (part, cols), 1)
    col_offset = jnp.where(col_lane < cols // 2, col_lane, col_lane - cols)
    row_lines[...] = tap_value(HALO - band_lane, row_bins[...]).astype(jnp.float32)
    col_lines[...] = tap_value(col_offset, col_bins[...]).astype(jnp.float32)
    square = (cols, cols)
    near = (
        jnp.abs(lax.broadcasted_iota(jnp.int32, square, 0) - lax.broadcasted_iota(jnp.int32, square, 1))
        <= HALO
    )

    def bands(i, carry):
        row_band = jnp.broadcast_to(row_lines[pl.ds(i, 1), :], (block, 2 * block))
        row_bands[i] = pltpu.roll(row_band, 0, 1, stride=1, stride_axis=0).astype(jnp.bfloat16)
        col_band = jnp.broadcast_to(col_lines[pl.ds(i, 1), :], square)
        col_band = pltpu.roll(col_band, 0, 1, stride=1, stride_axis=0)
        col_bands[i] = jnp.where(near, col_band, 0.0).astype(jnp.bfloat16)
        return carry

    lax.fori_loop(0, part, bands, 0)
    edge = jnp.zeros((chunks, size, rows, cols), jnp.bfloat16)
    received[:, 0] = edge
    received[:, n + 1] = edge

    to_after.wait_recv()
    to_before.wait_recv()
    mine = halo_out[pl.ds(HALO, rows), :]
    fill = jnp.zeros((rows - HALO, cols), jnp.float32)
    from_before = jnp.where(me > 0, halo_in[0], 0.0)
    from_after = jnp.where(me < n - 1, halo_in[1], 0.0)
    if rows > HALO:
        from_before = jnp.concatenate([from_before, fill], axis=0)
        from_after = jnp.concatenate([fill, from_after], axis=0)
    mine = mine + from_before + from_after
    sum_ref[...] = mine
    image[pl.ds(pl.multiple_of(me * rows, HALO), rows), :] = mine.astype(jnp.bfloat16)

    def image_copy(other, sender):
        place = pl.ds(pl.multiple_of(sender * rows, HALO), rows)
        return pltpu.make_async_remote_copy(
            src_ref=image.at[place],
            dst_ref=image.at[place],
            send_sem=image_send.at[other],
            recv_sem=image_recv.at[sender],
            device_id={"strip": other},
            device_id_type=MESH,
        )

    def send_image(step, carry):
        image_copy(partner(step), me).start()
        return carry

    lax.fori_loop(0, n - 1, send_image, 0)
    if chunks > 2:
        send_chunk(2)

    def align(chunk):
        def await_strip(step, inner):
            other = lax.rem(me + step, n)
            strip_copy(chunk, other, other, other).wait_recv()
            return inner

        lax.fori_loop(1, n, await_strip, 0)

        def one(index, inner):
            i = chunk * size + index
            row_band = row_bands[i][:, : block + 2 * HALO]
            col_band = col_bands[i]
            for start in range(0, height, block):
                window = received[chunk, pl.ds(start // rows, block // rows + 2), index]
                window = window.reshape(block + 2 * rows, cols)[rows - HALO : rows + block + HALO]
                moved = jnp.dot(row_band, window, preferred_element_type=jnp.float32)
                moved = jnp.dot(
                    moved.astype(jnp.bfloat16), col_band, preferred_element_type=jnp.float32
                )
                aligned_ref[i, pl.ds(start, block), :] = moved.astype(jnp.bfloat16)
            return inner

        lax.fori_loop(0, size, one, 0, unroll=True)

    for own_copy in own_copies:
        own_copy.wait()
    align(0)
    for chunk in range(3, chunks):
        await_left(chunk - 2)
        send_chunk(chunk)

    def await_image(step, carry):
        other = lax.rem(me + step, n)
        image_copy(other, other).wait_recv()
        return carry

    lax.fori_loop(1, n, await_image, 0)
    image_pad[pl.ds(0, SUB), :] = jnp.zeros((SUB, cols), jnp.float32)
    image_pad[pl.ds(SUB + height, SUB), :] = jnp.zeros((SUB, cols), jnp.float32)
    image_pad[pl.ds(SUB, height), :] = image[...].astype(jnp.float32)
    for a in range(WIDE):
        window = image_pad[pl.ds(SUB + a - LAGS, height), :]
        image_t[pl.ds(a * cols, cols), :] = window.T.astype(jnp.bfloat16)

    low_lane = lax.broadcasted_iota(jnp.int32, (SUB, cols), 1) < cols // 2
    tail_lane = lax.broadcasted_iota(jnp.int32, (SUB, cols), 1)
    tail_keep = (tail_lane < SUB) | (tail_lane >= cols // 2)
    pieces = cols // SUB

    def correlate(chunk):
        def pair(index, inner):
            first = chunk * size + 2 * index
            both = jnp.concatenate([aligned_ref[first], aligned_ref[first + 1]], axis=1)
            for a in range(WIDE):
                products = jnp.dot(
                    image_t[pl.ds(a * cols, cols), :], both, preferred_element_type=jnp.float32
                )
                for k in range(2):
                    total = None
                    for piece in range(pieces):
                        term = products[piece * SUB : (piece + 1) * SUB, k * cols : (k + 1) * cols]
                        if piece:
                            term = pltpu.roll(term, cols - piece * SUB, 1)
                        if piece == 0:
                            term = jnp.where(low_lane, term, 0.0)
                        elif piece == pieces - 1:
                            term = jnp.where(tail_keep, term, 0.0)
                        total = term if total is None else total + term
                    place = pl.multiple_of((a * part + first + k) * SUB, SUB)
                    diagonals[pl.ds(place, SUB), :] = total
            return inner

        lax.fori_loop(0, size // 2, pair, 0)

    correlate(0)

    def work_chunk(chunk, carry):
        align(chunk)
        correlate(chunk)
        return carry

    lax.fori_loop(1, chunks, work_chunk, 0)

    gathered = jnp.zeros((WIDE * part, cols), jnp.float32)
    for s in range(SUB):
        lines = diagonals[pl.ds(s, WIDE * part, stride=SUB), :]
        turn = (LAGS - s) % cols
        gathered = gathered + (pltpu.roll(lines, turn, 1) if turn else lines)
    lane_in = lax.broadcasted_iota(jnp.int32, square, 0)
    lane_out = lax.broadcasted_iota(jnp.int32, square, 1)
    mirror = ((lane_in + lane_out == 2 * LAGS) & (lane_out < WIDE)).astype(jnp.float32)
    gathered = jnp.dot(
        gathered, mirror, precision=lax.Precision.HIGHEST, preferred_element_type=jnp.float32
    )
    result = jnp.zeros((part, cols), jnp.float32)
    for a in range(WIDE):
        lags = gathered[a * part : (a + 1) * part, :]
        result = result + (pltpu.roll(lags, a * WIDE, 1) if a else lags)
    corr_out_ref[...] = (result * scaling)[:, : WIDE * WIDE]

    def drain(step, carry):
        image_copy(lax.rem(me + step, n), me).wait_send()
        return carry

    lax.fori_loop(1, n, drain, 0)
    for chunk in sorted({0, chunks - 1} | {min(c, chunks - 1) for c in (chunks - 2,) if c > 0}):
        await_left(chunk)
    to_after.wait_send()
    to_before.wait_send()


def write_out(*refs):
    copies = [pltpu.make_async_copy(refs[k], refs[3 + k], refs[6].at[k]) for k in range(3)]
    for copy in copies:
        copy.start()
    for copy in copies:
        copy.wait()


def on_device(data, response, pixel_ids, shift_bins):
    rows, cols, pixels = data.shape
    n = lax.axis_size("strip")
    part = pixels // n
    chunks = max(1, part // 4)
    height = n * rows
    block = min(128, height)
    reach = rows + 2 * HALO
    assert rows >= HALO and rows % 16 == 0 and block % rows == 0 and (part // chunks) % 2 == 0 and height % block == 0
    scaling = 1.0 / math.sqrt(pixels * height * cols)
    span = TAPS + (-TAPS) % SUB
    vmem = pl.BlockSpec(memory_space=pltpu.VMEM)
    hbm = pl.BlockSpec(memory_space=pltpu.HBM)
    bf16, f32 = jnp.bfloat16, jnp.float32
    shapes = (
        jax.ShapeDtypeStruct((part, height, cols), bf16),
        jax.ShapeDtypeStruct((rows, cols), f32),
        jax.ShapeDtypeStruct((part, WIDE * WIDE), f32),
    )
    results = pl.pallas_call(
        functools.partial(kernel, n, chunks, scaling),
        out_shape=shapes,
        in_specs=[hbm] * 4,
        out_specs=(vmem, vmem, vmem),
        scratch_shapes=[
            pltpu.VMEM((rows, cols, pixels), bf16),
            pltpu.VMEM((pixels, pixels), bf16),
            pltpu.VMEM((1, pixels), jnp.int32),
            pltpu.VMEM((2, pixels), jnp.int32),
            pltpu.SMEM((2, pixels), jnp.int32),
            pltpu.VMEM((pixels * rows, cols), f32),
            pltpu.VMEM((rows // 2, pixels, 2 * cols), bf16),
            pltpu.VMEM((pixels, rows, cols), bf16),
            pltpu.VMEM((chunks, n + 2, part // chunks, rows, cols), bf16),
            pltpu.VMEM((part, block, 2 * block), bf16),
            pltpu.VMEM((part, cols, cols), bf16),
            pltpu.VMEM((part, 2 * block), jnp.int32),
            pltpu.VMEM((part, cols), jnp.int32),
            pltpu.VMEM((part, 2 * block), f32),
            pltpu.VMEM((part, cols), f32),
            pltpu.VMEM((span, pixels), f32),
            pltpu.VMEM((span, pixels), f32),
            pltpu.VMEM((TAPS * span, pixels), bf16),
            pltpu.VMEM((TAPS, span + rows, cols), f32),
            pltpu.VMEM((reach, cols), f32),
            pltpu.VMEM((2, HALO, cols), f32),
            pltpu.VMEM((height, cols), bf16),
            pltpu.VMEM((height + 2 * SUB, cols), f32),
            pltpu.VMEM((WIDE * cols, height), bf16),
            pltpu.VMEM((WIDE * part * SUB, cols), f32),
            pltpu.SemaphoreType.DMA((chunks, n)),
            pltpu.SemaphoreType.DMA((chunks, n)),
            pltpu.SemaphoreType.DMA((2,)),
            pltpu.SemaphoreType.DMA((2,)),
            pltpu.SemaphoreType.DMA((n,)),
            pltpu.SemaphoreType.DMA((n,)),
            pltpu.SemaphoreType.DMA((chunks,)),
            pltpu.SemaphoreType.DMA((5,)),
        ],
        compiler_params=pltpu.CompilerParams(
            collective_id=0, has_side_effects=True, vmem_limit_bytes=48 * 1024 * 1024
        ),
    )(*(pltpu.with_memory_space_constraint(a, pltpu.HBM) for a in (data, response, pixel_ids.reshape(1, pixels), shift_bins)))
    return pl.pallas_call(
        write_out,
        out_shape=shapes,
        in_specs=[vmem] * 3,
        out_specs=(hbm, hbm, hbm),
        scratch_shapes=[pltpu.SemaphoreType.DMA((3,))],
        compiler_params=pltpu.CompilerParams(vmem_limit_bytes=8 * 1024 * 1024),
    )(*results)


def solution(mesh):
    placed = (P(("groups", "strip"), None, None), P(), P(), P())
    return jax.shard_map(
        on_device,
        mesh=mesh,
        in_specs=placed,
        out_specs=(
            P("strip", "groups", None),
            P(("groups", "strip"), None),
            P(("groups", "strip"), None),
        ),
        check_vma=False,
    )
```

```python
import functools
import math

import jax
import jax.numpy as jnp
from jax import lax
from jax.experimental import pallas as pl
from jax.experimental.pallas import tpu as pltpu
from jax.sharding import PartitionSpec as P

HALO = 16
LAGS = 4
TAPS = 2 * HALO + 1
WIDE = 2 * LAGS + 1
SUB = 8
MESH = pl.DeviceIdType.MESH


def tap_value(offset, bins):
    u = offset.astype(jnp.float32) - bins.astype(jnp.float32) / 4.0
    angle = jnp.pi * u
    safe = jnp.where(u == 0.0, 1.0, angle)
    sinc = jnp.where(u == 0.0, 1.0, jnp.sin(safe) / safe)
    value = sinc * (0.5 + 0.5 * jnp.cos(angle / (HALO + 1)))
    inside = (jnp.abs(u) < HALO + 1) & (jnp.abs(offset) <= HALO)
    return jnp.where(inside, value, 0.0).astype(jnp.bfloat16)


def kernel(
    n, chunks, scaling,
    data_hbm, resp_hbm, ids_hbm, bins_hbm,
    aligned_ref, sum_ref, corr_out_ref,
    data_ref, resp_ref, ids_ref, bins_ref, bins_smem,
    chosen_t, spread, natural, corrected, received, row_bands, col_bands, row_bins, col_bins,
    row_lines, col_lines, row_taps, col_taps, outer_taps,
    totals, halo_out, halo_in, image, image_pad, image_t, diagonals,
    send_sems, recv_sems, halo_send, halo_recv, image_send, image_recv, own_sem, load_sems,
):
    rows, cols, pixels = data_ref.shape
    half_rows = rows // 2
    part = pixels // n
    size = part // chunks
    height = n * rows
    block = min(128, height)
    reach = rows + 2 * HALO
    span = TAPS + (-TAPS) % SUB
    me = lax.axis_index("strip")

    loads = [
        pltpu.make_async_copy(source, target, load_sems.at[k])
        for k, (source, target) in enumerate(
            (
                (resp_hbm, resp_ref),
                (ids_hbm, ids_ref),
                (data_hbm, data_ref),
                (bins_hbm, bins_ref),
                (bins_hbm, bins_smem),
            )
        )
    ]
    for load in loads:
        load.start()

    barrier = pltpu.get_barrier_semaphore()

    def greet(t, carry):
        other = lax.rem(me + t, n)
        pl.semaphore_signal(barrier, inc=1, device_id={"strip": other}, device_id_type=MESH)
        return carry

    lax.fori_loop(1, n, greet, 0)

    loads[0].wait()
    loads[1].wait()
    pick = lax.broadcasted_iota(jnp.int32, (pixels, pixels), 0) == ids_ref[...]
    chosen = jnp.dot(
        resp_ref[...], pick.astype(jnp.float32).astype(jnp.bfloat16), preferred_element_type=jnp.float32
    )
    chosen_t[...] = chosen.T.astype(jnp.bfloat16)
    loads[2].wait()

    def correct(first, count):
        first = pl.multiple_of(first, 16)
        for y in range(half_rows):
            both_rows = jnp.concatenate([data_ref[y], data_ref[y + half_rows]], axis=0)
            pair_rows = lax.dot_general(
                chosen_t[pl.ds(first, count), :],
                both_rows,
                (((1,), (1,)), ((), ())),
                preferred_element_type=jnp.float32,
            )
            natural[y, pl.ds(first, count), :] = pair_rows.astype(jnp.bfloat16)
            spread[pl.ds(first * rows + y, count, stride=rows), :] = pair_rows[:, :cols]
            spread[pl.ds(first * rows + y + half_rows, count, stride=rows), :] = pair_rows[:, cols:]
        flat = spread[pl.ds(pl.multiple_of(first * rows, 16), count * rows), :]
        corrected[pl.ds(first, count)] = flat.reshape(count, rows, cols).astype(jnp.bfloat16)

    def strip_copy(chunk, other, owner, sender):
        return pltpu.make_async_remote_copy(
            src_ref=corrected.at[pl.ds(owner * part + chunk * size, size)],
            dst_ref=received.at[chunk, sender + 1],
            send_sem=send_sems.at[chunk, other],
            recv_sem=recv_sems.at[chunk, sender],
            device_id={"strip": other},
            device_id_type=MESH,
        )

    def partner(step):
        half = lax.div(step + 1, 2)
        even = lax.rem(step, 2) == 0
        if n & (n - 1):
            return lax.rem(me + n // 2 + jnp.where(even, half, -half), n)
        return me ^ jnp.where(even, n // 2 + half, half)

    def send_chunk(chunk):
        def one(step, carry):
            other = partner(step)
            strip_copy(chunk, other, other, me).start()
            return carry

        lax.fori_loop(0, n - 1, one, 0)

    def await_left(chunk):
        def one(step, carry):
            other = partner(step)
            strip_copy(chunk, other, other, me).wait_send()
            return carry

        lax.fori_loop(0, n - 1, one, 0)

    early = min(2, chunks)
    if n & (n - 1) or n < 4:
        correct(0, pixels)
        pl.semaphore_wait(barrier, n - 1)
        for chunk in range(early):
            send_chunk(chunk)
    else:
        side = lax.div(me, n // 2)
        correct((1 - side) * (pixels // 2), pixels // 2)
        pl.semaphore_wait(barrier, n - 1)

        def send_far(step, carry):
            other = me ^ (n // 2 + step)
            strip_copy(0, other, other, me).start()
            return carry

        def send_near(step, carry):
            other = me ^ step
            strip_copy(0, other, other, me).start()
            return carry

        lax.fori_loop(0, n // 2, send_far, 0)
        correct(side * (pixels // 2), pixels // 2)
        lax.fori_loop(1, n // 2, send_near, 0)
        for chunk in range(1, early):
            send_chunk(chunk)
    own_copies = [
        pltpu.make_async_copy(
            corrected.at[pl.ds(me * part + chunk * size, size)],
            received.at[chunk, me + 1],
            own_sem.at[chunk],
        )
        for chunk in range(chunks)
    ]
    for own_copy in own_copies:
        own_copy.start()

    loads[3].wait()
    loads[4].wait()
    taps_at = lax.broadcasted_iota(jnp.int32, (span, pixels), 0) - HALO
    row_taps[...] = tap_value(taps_at, bins_ref[0:1, :]).astype(jnp.float32)
    col_taps[...] = tap_value(taps_at, bins_ref[1:2, :]).astype(jnp.float32)
    totals[...] = jnp.zeros_like(totals)
    outer = row_taps[...].reshape(1, span, pixels) * col_taps[pl.ds(0, TAPS), :].reshape(TAPS, 1, pixels)
    outer_taps[...] = outer.reshape(TAPS * span, pixels).astype(jnp.bfloat16)
    gap = jnp.zeros((TAPS, half_rows, cols), jnp.float32)
    for y in range(half_rows):
        terms = jnp.dot(outer_taps[...], natural[y], preferred_element_type=jnp.float32)
        terms = terms.reshape(TAPS, span, 2 * cols)
        terms = jnp.concatenate([terms[:, :, :cols], gap], axis=1) + jnp.concatenate(
            [gap, terms[:, :, cols:]], axis=1
        )
        totals[:, pl.ds(y, span + half_rows), :] += terms
    lane = lax.broadcasted_iota(jnp.int32, (reach, cols), 1)
    share = jnp.zeros((reach, cols), jnp.float32)
    for j in range(TAPS):
        shift = j - HALO
        moved = totals[j, pl.ds(0, reach), :]
        if shift:
            moved = pltpu.roll(moved, shift % cols, 1)
            source = lane - shift
            moved = jnp.where((source >= 0) & (source < cols), moved, 0.0)
        share = share + moved
    halo_out[...] = share

    before, after = lax.rem(me + n - 1, n), lax.rem(me + 1, n)

    def halo_copy(side, other, start):
        return pltpu.make_async_remote_copy(
            src_ref=halo_out.at[pl.ds(start, HALO)],
            dst_ref=halo_in.at[side],
            send_sem=halo_send.at[side],
            recv_sem=halo_recv.at[side],
            device_id={"strip": other},
            device_id_type=MESH,
        )

    to_after = halo_copy(0, after, HALO + rows)
    to_before = halo_copy(1, before, 0)
    to_after.start()
    to_before.start()
    middle = min(4, chunks)
    for chunk in range(early, middle):
        send_chunk(chunk)
    for i in range(part):
        row_bins[pl.ds(i, 1), :] = jnp.full((1, 2 * block), bins_smem[0, me * part + i], jnp.int32)
        col_bins[pl.ds(i, 1), :] = jnp.full((1, cols), bins_smem[1, me * part + i], jnp.int32)
    band_lane = lax.broadcasted_iota(jnp.int32, (part, 2 * block), 1)
    col_lane = lax.broadcasted_iota(jnp.int32, (part, cols), 1)
    col_offset = jnp.where(col_lane < cols // 2, col_lane, col_lane - cols)
    row_lines[...] = tap_value(HALO - band_lane, row_bins[...]).astype(jnp.float32)
    col_lines[...] = tap_value(col_offset, col_bins[...]).astype(jnp.float32)
    square = (cols, cols)
    near = (
        jnp.abs(lax.broadcasted_iota(jnp.int32, square, 0) - lax.broadcasted_iota(jnp.int32, square, 1))
        <= HALO
    )

    def bands(i, carry):
        row_band = jnp.broadcast_to(row_lines[pl.ds(i, 1), :], (block, 2 * block))
        row_bands[i] = pltpu.roll(row_band, 0, 1, stride=1, stride_axis=0).astype(jnp.bfloat16)
        col_band = jnp.broadcast_to(col_lines[pl.ds(i, 1), :], square)
        col_band = pltpu.roll(col_band, 0, 1, stride=1, stride_axis=0)
        col_bands[i] = jnp.where(near, col_band, 0.0).astype(jnp.bfloat16)
        return carry

    lax.fori_loop(0, part, bands, 0)
    edge = jnp.zeros((chunks, size, rows, cols), jnp.bfloat16)
    received[:, 0] = edge
    received[:, n + 1] = edge

    to_after.wait_recv()
    to_before.wait_recv()
    mine = halo_out[pl.ds(HALO, rows), :]
    fill = jnp.zeros((rows - HALO, cols), jnp.float32)
    from_before = jnp.where(me > 0, halo_in[0], 0.0)
    from_after = jnp.where(me < n - 1, halo_in[1], 0.0)
    if rows > HALO:
        from_before = jnp.concatenate([from_before, fill], axis=0)
        from_after = jnp.concatenate([fill, from_after], axis=0)
    mine = mine + from_before + from_after
    sum_ref[...] = mine
    image[pl.ds(pl.multiple_of(me * rows, HALO), rows), :] = mine.astype(jnp.bfloat16)

    def image_copy(other, sender):
        place = pl.ds(pl.multiple_of(sender * rows, HALO), rows)
        return pltpu.make_async_remote_copy(
            src_ref=image.at[place],
            dst_ref=image.at[place],
            send_sem=image_send.at[other],
            recv_sem=image_recv.at[sender],
            device_id={"strip": other},
            device_id_type=MESH,
        )

    def send_image(step, carry):
        image_copy(partner(step), me).start()
        return carry

    lax.fori_loop(0, n - 1, send_image, 0)
    for chunk in range(middle, chunks):
        send_chunk(chunk)

    def align(chunk):
        def await_strip(step, inner):
            other = lax.rem(me + step, n)
            strip_copy(chunk, other, other, other).wait_recv()
            return inner

        lax.fori_loop(1, n, await_strip, 0)

        def one(index, inner):
            i = chunk * size + index
            row_band = row_bands[i][:, : block + 2 * HALO]
            col_band = col_bands[i]
            for start in range(0, height, block):
                window = received[chunk, pl.ds(start // rows, block // rows + 2), index]
                window = window.reshape(block + 2 * rows, cols)[rows - HALO : rows + block + HALO]
                moved = jnp.dot(row_band, window, preferred_element_type=jnp.float32)
                moved = jnp.dot(
                    moved.astype(jnp.bfloat16), col_band, preferred_element_type=jnp.float32
                )
                aligned_ref[i, pl.ds(start, block), :] = moved.astype(jnp.bfloat16)
            return inner

        lax.fori_loop(0, size, one, 0, unroll=True)

    for own_copy in own_copies:
        own_copy.wait()
    align(0)

    def await_image(step, carry):
        other = lax.rem(me + step, n)
        image_copy(other, other).wait_recv()
        return carry

    lax.fori_loop(1, n, await_image, 0)
    image_pad[pl.ds(0, SUB), :] = jnp.zeros((SUB, cols), jnp.float32)
    image_pad[pl.ds(SUB + height, SUB), :] = jnp.zeros((SUB, cols), jnp.float32)
    image_pad[pl.ds(SUB, height), :] = image[...].astype(jnp.float32)
    for a in range(WIDE):
        window = image_pad[pl.ds(SUB + a - LAGS, height), :]
        image_t[pl.ds(a * cols, cols), :] = window.T.astype(jnp.bfloat16)

    low_lane = lax.broadcasted_iota(jnp.int32, (SUB, cols), 1) < cols // 2
    tail_lane = lax.broadcasted_iota(jnp.int32, (SUB, cols), 1)
    tail_keep = (tail_lane < SUB) | (tail_lane >= cols // 2)
    pieces = cols // SUB

    def correlate(chunk):
        def pair(index, inner):
            first = chunk * size + 2 * index
            both = jnp.concatenate([aligned_ref[first], aligned_ref[first + 1]], axis=1)
            for a in range(WIDE):
                products = jnp.dot(
                    image_t[pl.ds(a * cols, cols), :], both, preferred_element_type=jnp.float32
                )
                for k in range(2):
                    total = None
                    for piece in range(pieces):
                        term = products[piece * SUB : (piece + 1) * SUB, k * cols : (k + 1) * cols]
                        if piece:
                            term = pltpu.roll(term, cols - piece * SUB, 1)
                        if piece == 0:
                            term = jnp.where(low_lane, term, 0.0)
                        elif piece == pieces - 1:
                            term = jnp.where(tail_keep, term, 0.0)
                        total = term if total is None else total + term
                    place = pl.multiple_of((a * part + first + k) * SUB, SUB)
                    diagonals[pl.ds(place, SUB), :] = total
            return inner

        lax.fori_loop(0, size // 2, pair, 0)

    correlate(0)

    def work_chunk(chunk, carry):
        align(chunk)
        correlate(chunk)
        return carry

    lax.fori_loop(1, chunks, work_chunk, 0)

    gathered = jnp.zeros((WIDE * part, cols), jnp.float32)
    for s in range(SUB):
        lines = diagonals[pl.ds(s, WIDE * part, stride=SUB), :]
        turn = (LAGS - s) % cols
        gathered = gathered + (pltpu.roll(lines, turn, 1) if turn else lines)
    lane_in = lax.broadcasted_iota(jnp.int32, square, 0)
    lane_out = lax.broadcasted_iota(jnp.int32, square, 1)
    mirror = ((lane_in + lane_out == 2 * LAGS) & (lane_out < WIDE)).astype(jnp.float32)
    gathered = jnp.dot(
        gathered, mirror, precision=lax.Precision.HIGHEST, preferred_element_type=jnp.float32
    )
    result = jnp.zeros((part, cols), jnp.float32)
    for a in range(WIDE):
        lags = gathered[a * part : (a + 1) * part, :]
        result = result + (pltpu.roll(lags, a * WIDE, 1) if a else lags)
    corr_out_ref[...] = (result * scaling)[:, : WIDE * WIDE]

    def drain(step, carry):
        image_copy(lax.rem(me + step, n), me).wait_send()
        return carry

    lax.fori_loop(1, n, drain, 0)
    for chunk in range(chunks):
        await_left(chunk)
    to_after.wait_send()
    to_before.wait_send()


def write_out(*refs):
    copies = [pltpu.make_async_copy(refs[k], refs[3 + k], refs[6].at[k]) for k in range(3)]
    for copy in copies:
        copy.start()
    for copy in copies:
        copy.wait()


def on_device(data, response, pixel_ids, shift_bins):
    rows, cols, pixels = data.shape
    n = lax.axis_size("strip")
    part = pixels // n
    chunks = max(1, part // 2)
    height = n * rows
    block = min(128, height)
    reach = rows + 2 * HALO
    assert rows >= HALO and rows % 16 == 0 and block % rows == 0 and (part // chunks) % 2 == 0 and height % block == 0
    scaling = 1.0 / math.sqrt(pixels * height * cols)
    span = TAPS + (-TAPS) % SUB
    vmem = pl.BlockSpec(memory_space=pltpu.VMEM)
    hbm = pl.BlockSpec(memory_space=pltpu.HBM)
    bf16, f32 = jnp.bfloat16, jnp.float32
    shapes = (
        jax.ShapeDtypeStruct((part, height, cols), bf16),
        jax.ShapeDtypeStruct((rows, cols), f32),
        jax.ShapeDtypeStruct((part, WIDE * WIDE), f32),
    )
    results = pl.pallas_call(
        functools.partial(kernel, n, chunks, scaling),
        out_shape=shapes,
        in_specs=[hbm] * 4,
        out_specs=(vmem, vmem, vmem),
        scratch_shapes=[
            pltpu.VMEM((rows, cols, pixels), bf16),
            pltpu.VMEM((pixels, pixels), bf16),
            pltpu.VMEM((1, pixels), jnp.int32),
            pltpu.VMEM((2, pixels), jnp.int32),
            pltpu.SMEM((2, pixels), jnp.int32),
            pltpu.VMEM((pixels, pixels), bf16),
            pltpu.VMEM((pixels * rows, cols), f32),
            pltpu.VMEM((rows // 2, pixels, 2 * cols), bf16),
            pltpu.VMEM((pixels, rows, cols), bf16),
            pltpu.VMEM((chunks, n + 2, part // chunks, rows, cols), bf16),
            pltpu.VMEM((part, block, 2 * block), bf16),
            pltpu.VMEM((part, cols, cols), bf16),
            pltpu.VMEM((part, 2 * block), jnp.int32),
            pltpu.VMEM((part, cols), jnp.int32),
            pltpu.VMEM((part, 2 * block), f32),
            pltpu.VMEM((part, cols), f32),
            pltpu.VMEM((span, pixels), f32),
            pltpu.VMEM((span, pixels), f32),
            pltpu.VMEM((TAPS * span, pixels), bf16),
            pltpu.VMEM((TAPS, span + rows, cols), f32),
            pltpu.VMEM((reach, cols), f32),
            pltpu.VMEM((2, HALO, cols), f32),
            pltpu.VMEM((height, cols), bf16),
            pltpu.VMEM((height + 2 * SUB, cols), f32),
            pltpu.VMEM((WIDE * cols, height), bf16),
            pltpu.VMEM((WIDE * part * SUB, cols), f32),
            pltpu.SemaphoreType.DMA((chunks, n)),
            pltpu.SemaphoreType.DMA((chunks, n)),
            pltpu.SemaphoreType.DMA((2,)),
            pltpu.SemaphoreType.DMA((2,)),
            pltpu.SemaphoreType.DMA((n,)),
            pltpu.SemaphoreType.DMA((n,)),
            pltpu.SemaphoreType.DMA((chunks,)),
            pltpu.SemaphoreType.DMA((5,)),
        ],
        compiler_params=pltpu.CompilerParams(
            collective_id=0, has_side_effects=True, vmem_limit_bytes=48 * 1024 * 1024
        ),
    )(*(pltpu.with_memory_space_constraint(a, pltpu.HBM) for a in (data, response, pixel_ids.reshape(1, pixels), shift_bins)))
    return pl.pallas_call(
        write_out,
        out_shape=shapes,
        in_specs=[vmem] * 3,
        out_specs=(hbm, hbm, hbm),
        scratch_shapes=[pltpu.SemaphoreType.DMA((3,))],
        compiler_params=pltpu.CompilerParams(vmem_limit_bytes=8 * 1024 * 1024),
    )(*results)


def solution(mesh):
    placed = (P(("groups", "strip"), None, None), P(), P(), P())
    return jax.shard_map(
        on_device,
        mesh=mesh,
        in_specs=placed,
        out_specs=(
            P("strip", "groups", None),
            P(("groups", "strip"), None),
            P(("groups", "strip"), None),
        ),
        check_vma=False,
    )
```

```python
import functools
import math

import jax
import jax.numpy as jnp
from jax import lax
from jax.experimental import pallas as pl
from jax.experimental.pallas import tpu as pltpu
from jax.sharding import PartitionSpec as P

HALO = 16
LAGS = 4
TAPS = 2 * HALO + 1
WIDE = 2 * LAGS + 1
SUB = 8
MESH = pl.DeviceIdType.MESH


def tap_value(offset, bins):
    u = offset.astype(jnp.float32) - bins.astype(jnp.float32) / 4.0
    angle = jnp.pi * u
    safe = jnp.where(u == 0.0, 1.0, angle)
    sinc = jnp.where(u == 0.0, 1.0, jnp.sin(safe) / safe)
    value = sinc * (0.5 + 0.5 * jnp.cos(angle / (HALO + 1)))
    inside = (jnp.abs(u) < HALO + 1) & (jnp.abs(offset) <= HALO)
    return jnp.where(inside, value, 0.0).astype(jnp.bfloat16)


def kernel(
    n, chunks, scaling,
    data_hbm, resp_hbm, ids_hbm, bins_hbm,
    aligned_ref, sum_ref, corr_out_ref,
    data_ref, resp_ref, ids_ref, bins_ref, bins_smem,
    chosen_t, spread, natural, corrected, received, row_bands, col_bands, row_bins, col_bins,
    row_lines, col_lines, row_taps, col_taps, outer_taps,
    totals, halo_out, halo_in, image, image_pad, image_t, diagonals,
    send_sems, recv_sems, halo_send, halo_recv, image_send, image_recv, own_sem, load_sems,
):
    rows, cols, pixels = data_ref.shape
    half_rows = rows // 2
    part = pixels // n
    size = part // chunks
    height = n * rows
    block = min(128, height)
    reach = rows + 2 * HALO
    span = TAPS + (-TAPS) % SUB
    me = lax.axis_index("strip")

    loads = [
        pltpu.make_async_copy(source, target, load_sems.at[k])
        for k, (source, target) in enumerate(
            (
                (resp_hbm, resp_ref),
                (ids_hbm, ids_ref),
                (data_hbm, data_ref),
                (bins_hbm, bins_ref),
                (bins_hbm, bins_smem),
            )
        )
    ]
    for load in loads:
        load.start()

    barrier = pltpu.get_barrier_semaphore()

    def greet(t, carry):
        other = lax.rem(me + t, n)
        pl.semaphore_signal(barrier, inc=1, device_id={"strip": other}, device_id_type=MESH)
        return carry

    lax.fori_loop(1, n, greet, 0)

    loads[0].wait()
    loads[1].wait()
    pick = lax.broadcasted_iota(jnp.int32, (pixels, pixels), 0) == ids_ref[...]
    chosen = jnp.dot(
        resp_ref[...], pick.astype(jnp.float32).astype(jnp.bfloat16), preferred_element_type=jnp.float32
    )
    chosen_t[...] = chosen.T.astype(jnp.bfloat16)
    loads[2].wait()

    def correct(first, count):
        first = pl.multiple_of(first, 16)
        for y in range(half_rows):
            both_rows = jnp.concatenate([data_ref[y], data_ref[y + half_rows]], axis=0)
            pair_rows = lax.dot_general(
                chosen_t[pl.ds(first, count), :],
                both_rows,
                (((1,), (1,)), ((), ())),
                preferred_element_type=jnp.float32,
            )
            natural[y, pl.ds(first, count), :] = pair_rows.astype(jnp.bfloat16)
            spread[pl.ds(first * rows + y, count, stride=rows), :] = pair_rows[:, :cols]
            spread[pl.ds(first * rows + y + half_rows, count, stride=rows), :] = pair_rows[:, cols:]
        flat = spread[pl.ds(pl.multiple_of(first * rows, 16), count * rows), :]
        corrected[pl.ds(first, count)] = flat.reshape(count, rows, cols).astype(jnp.bfloat16)

    def strip_copy(chunk, other, owner, sender):
        return pltpu.make_async_remote_copy(
            src_ref=corrected.at[pl.ds(owner * part + chunk * size, size)],
            dst_ref=received.at[chunk, sender + 1],
            send_sem=send_sems.at[chunk, other],
            recv_sem=recv_sems.at[chunk, sender],
            device_id={"strip": other},
            device_id_type=MESH,
        )

    def partner(step):
        half = lax.div(step + 1, 2)
        even = lax.rem(step, 2) == 0
        if n & (n - 1):
            return lax.rem(me + n // 2 + jnp.where(even, half, -half), n)
        return me ^ jnp.where(even, n // 2 + half, half)

    def send_chunk(chunk):
        def one(step, carry):
            other = partner(step)
            strip_copy(chunk, other, other, me).start()
            return carry

        lax.fori_loop(0, n - 1, one, 0)

    def await_left(chunk):
        def one(step, carry):
            other = partner(step)
            strip_copy(chunk, other, other, me).wait_send()
            return carry

        lax.fori_loop(0, n - 1, one, 0)

    early = 1
    if n & (n - 1) or n < 4:
        correct(0, pixels)
        pl.semaphore_wait(barrier, n - 1)
        for chunk in range(early):
            send_chunk(chunk)
    else:
        side = lax.div(me, n // 2)
        correct((1 - side) * (pixels // 2), pixels // 2)
        pl.semaphore_wait(barrier, n - 1)

        def send_far(step, carry):
            other = me ^ (n // 2 + step)
            strip_copy(0, other, other, me).start()
            return carry

        def send_near(step, carry):
            other = me ^ step
            strip_copy(0, other, other, me).start()
            return carry

        lax.fori_loop(0, n // 2, send_far, 0)
        correct(side * (pixels // 2), pixels // 2)
        lax.fori_loop(1, n // 2, send_near, 0)
        for chunk in range(1, early):
            send_chunk(chunk)
    own_copies = [
        pltpu.make_async_copy(
            corrected.at[pl.ds(me * part + chunk * size, size)],
            received.at[chunk, me + 1],
            own_sem.at[chunk],
        )
        for chunk in range(chunks)
    ]
    for own_copy in own_copies:
        own_copy.start()

    loads[3].wait()
    loads[4].wait()
    taps_at = lax.broadcasted_iota(jnp.int32, (span, pixels), 0) - HALO
    row_taps[...] = tap_value(taps_at, bins_ref[0:1, :]).astype(jnp.float32)
    col_taps[...] = tap_value(taps_at, bins_ref[1:2, :]).astype(jnp.float32)
    totals[...] = jnp.zeros_like(totals)
    outer = row_taps[...].reshape(1, span, pixels) * col_taps[pl.ds(0, TAPS), :].reshape(TAPS, 1, pixels)
    outer_taps[...] = outer.reshape(TAPS * span, pixels).astype(jnp.bfloat16)
    gap = jnp.zeros((TAPS, half_rows, cols), jnp.float32)
    for y in range(half_rows):
        terms = jnp.dot(outer_taps[...], natural[y], preferred_element_type=jnp.float32)
        terms = terms.reshape(TAPS, span, 2 * cols)
        terms = jnp.concatenate([terms[:, :, :cols], gap], axis=1) + jnp.concatenate(
            [gap, terms[:, :, cols:]], axis=1
        )
        totals[:, pl.ds(y, span + half_rows), :] += terms
    lane = lax.broadcasted_iota(jnp.int32, (reach, cols), 1)
    share = jnp.zeros((reach, cols), jnp.float32)
    for j in range(TAPS):
        shift = j - HALO
        moved = totals[j, pl.ds(0, reach), :]
        if shift:
            moved = pltpu.roll(moved, shift % cols, 1)
            source = lane - shift
            moved = jnp.where((source >= 0) & (source < cols), moved, 0.0)
        share = share + moved
    halo_out[...] = share

    before, after = lax.rem(me + n - 1, n), lax.rem(me + 1, n)

    def halo_copy(side, other, start):
        return pltpu.make_async_remote_copy(
            src_ref=halo_out.at[pl.ds(start, HALO)],
            dst_ref=halo_in.at[side],
            send_sem=halo_send.at[side],
            recv_sem=halo_recv.at[side],
            device_id={"strip": other},
            device_id_type=MESH,
        )

    to_after = halo_copy(0, after, HALO + rows)
    to_before = halo_copy(1, before, 0)
    to_after.start()
    to_before.start()
    middle = min(2, chunks)
    late = min(3, chunks)
    for chunk in range(early, middle):
        send_chunk(chunk)
    for i in range(part):
        row_bins[pl.ds(i, 1), :] = jnp.full((1, 2 * block), bins_smem[0, me * part + i], jnp.int32)
        col_bins[pl.ds(i, 1), :] = jnp.full((1, cols), bins_smem[1, me * part + i], jnp.int32)
    band_lane = lax.broadcasted_iota(jnp.int32, (part, 2 * block), 1)
    col_lane = lax.broadcasted_iota(jnp.int32, (part, cols), 1)
    col_offset = jnp.where(col_lane < cols // 2, col_lane, col_lane - cols)
    row_lines[...] = tap_value(HALO - band_lane, row_bins[...]).astype(jnp.float32)
    col_lines[...] = tap_value(col_offset, col_bins[...]).astype(jnp.float32)
    square = (cols, cols)
    near = (
        jnp.abs(lax.broadcasted_iota(jnp.int32, square, 0) - lax.broadcasted_iota(jnp.int32, square, 1))
        <= HALO
    )

    def bands(i, carry):
        row_band = jnp.broadcast_to(row_lines[pl.ds(i, 1), :], (block, 2 * block))
        row_bands[i] = pltpu.roll(row_band, 0, 1, stride=1, stride_axis=0).astype(jnp.bfloat16)
        col_band = jnp.broadcast_to(col_lines[pl.ds(i, 1), :], square)
        col_band = pltpu.roll(col_band, 0, 1, stride=1, stride_axis=0)
        col_bands[i] = jnp.where(near, col_band, 0.0).astype(jnp.bfloat16)
        return carry

    lax.fori_loop(0, part, bands, 0)
    edge = jnp.zeros((chunks, size, rows, cols), jnp.bfloat16)
    received[:, 0] = edge
    received[:, n + 1] = edge

    to_after.wait_recv()
    to_before.wait_recv()
    mine = halo_out[pl.ds(HALO, rows), :]
    fill = jnp.zeros((rows - HALO, cols), jnp.float32)
    from_before = jnp.where(me > 0, halo_in[0], 0.0)
    from_after = jnp.where(me < n - 1, halo_in[1], 0.0)
    if rows > HALO:
        from_before = jnp.concatenate([from_before, fill], axis=0)
        from_after = jnp.concatenate([fill, from_after], axis=0)
    mine = mine + from_before + from_after
    sum_ref[...] = mine
    image[pl.ds(pl.multiple_of(me * rows, HALO), rows), :] = mine.astype(jnp.bfloat16)

    def image_copy(other, sender):
        place = pl.ds(pl.multiple_of(sender * rows, HALO), rows)
        return pltpu.make_async_remote_copy(
            src_ref=image.at[place],
            dst_ref=image.at[place],
            send_sem=image_send.at[other],
            recv_sem=image_recv.at[sender],
            device_id={"strip": other},
            device_id_type=MESH,
        )

    def send_image(step, carry):
        image_copy(partner(step), me).start()
        return carry

    lax.fori_loop(0, n - 1, send_image, 0)
    for chunk in range(middle, late):
        send_chunk(chunk)

    def align(chunk):
        def await_strip(step, inner):
            other = lax.rem(me + step, n)
            strip_copy(chunk, other, other, other).wait_recv()
            return inner

        lax.fori_loop(1, n, await_strip, 0)

        def one(index, inner):
            i = chunk * size + index
            row_band = row_bands[i][:, : block + 2 * HALO]
            col_band = col_bands[i]
            for start in range(0, height, block):
                window = received[chunk, pl.ds(start // rows, block // rows + 2), index]
                window = window.reshape(block + 2 * rows, cols)[rows - HALO : rows + block + HALO]
                moved = jnp.dot(row_band, window, preferred_element_type=jnp.float32)
                moved = jnp.dot(
                    moved.astype(jnp.bfloat16), col_band, preferred_element_type=jnp.float32
                )
                aligned_ref[i, pl.ds(start, block), :] = moved.astype(jnp.bfloat16)
            return inner

        lax.fori_loop(0, size, one, 0, unroll=True)

    for own_copy in own_copies:
        own_copy.wait()
    align(0)
    for chunk in range(late, chunks):
        await_left(chunk - 2)
        send_chunk(chunk)

    def await_image(step, carry):
        other = lax.rem(me + step, n)
        image_copy(other, other).wait_recv()
        return carry

    lax.fori_loop(1, n, await_image, 0)
    image_pad[pl.ds(0, SUB), :] = jnp.zeros((SUB, cols), jnp.float32)
    image_pad[pl.ds(SUB + height, SUB), :] = jnp.zeros((SUB, cols), jnp.float32)
    image_pad[pl.ds(SUB, height), :] = image[...].astype(jnp.float32)
    for a in range(WIDE):
        window = image_pad[pl.ds(SUB + a - LAGS, height), :]
        image_t[pl.ds(a * cols, cols), :] = window.T.astype(jnp.bfloat16)

    low_lane = lax.broadcasted_iota(jnp.int32, (SUB, cols), 1) < cols // 2
    tail_lane = lax.broadcasted_iota(jnp.int32, (SUB, cols), 1)
    tail_keep = (tail_lane < SUB) | (tail_lane >= cols // 2)
    pieces = cols // SUB

    def correlate(chunk):
        def pair(index, inner):
            first = chunk * size + 2 * index
            both = jnp.concatenate([aligned_ref[first], aligned_ref[first + 1]], axis=1)
            for a in range(WIDE):
                products = jnp.dot(
                    image_t[pl.ds(a * cols, cols), :], both, preferred_element_type=jnp.float32
                )
                for k in range(2):
                    total = None
                    for piece in range(pieces):
                        term = products[piece * SUB : (piece + 1) * SUB, k * cols : (k + 1) * cols]
                        if piece:
                            term = pltpu.roll(term, cols - piece * SUB, 1)
                        if piece == 0:
                            term = jnp.where(low_lane, term, 0.0)
                        elif piece == pieces - 1:
                            term = jnp.where(tail_keep, term, 0.0)
                        total = term if total is None else total + term
                    place = pl.multiple_of((a * part + first + k) * SUB, SUB)
                    diagonals[pl.ds(place, SUB), :] = total
            return inner

        lax.fori_loop(0, size // 2, pair, 0)

    correlate(0)

    def work_chunk(chunk, carry):
        align(chunk)
        correlate(chunk)
        return carry

    lax.fori_loop(1, chunks, work_chunk, 0)

    gathered = jnp.zeros((WIDE * part, cols), jnp.float32)
    for s in range(SUB):
        lines = diagonals[pl.ds(s, WIDE * part, stride=SUB), :]
        turn = (LAGS - s) % cols
        gathered = gathered + (pltpu.roll(lines, turn, 1) if turn else lines)
    lane_in = lax.broadcasted_iota(jnp.int32, square, 0)
    lane_out = lax.broadcasted_iota(jnp.int32, square, 1)
    mirror = ((lane_in + lane_out == 2 * LAGS) & (lane_out < WIDE)).astype(jnp.float32)
    gathered = jnp.dot(
        gathered, mirror, precision=lax.Precision.HIGHEST, preferred_element_type=jnp.float32
    )
    result = jnp.zeros((part, cols), jnp.float32)
    for a in range(WIDE):
        lags = gathered[a * part : (a + 1) * part, :]
        result = result + (pltpu.roll(lags, a * WIDE, 1) if a else lags)
    corr_out_ref[...] = (result * scaling)[:, : WIDE * WIDE]

    def drain(step, carry):
        image_copy(lax.rem(me + step, n), me).wait_send()
        return carry

    lax.fori_loop(1, n, drain, 0)
    for chunk in range(chunks):
        if not late - 2 <= chunk < chunks - 2 or chunks == late:
            await_left(chunk)
    to_after.wait_send()
    to_before.wait_send()


def write_out(*refs):
    copies = [pltpu.make_async_copy(refs[k], refs[3 + k], refs[6].at[k]) for k in range(3)]
    for copy in copies:
        copy.start()
    for copy in copies:
        copy.wait()


def on_device(data, response, pixel_ids, shift_bins):
    rows, cols, pixels = data.shape
    n = lax.axis_size("strip")
    part = pixels // n
    chunks = max(1, part // 4)
    height = n * rows
    block = min(128, height)
    reach = rows + 2 * HALO
    assert rows >= HALO and rows % 16 == 0 and block % rows == 0 and (part // chunks) % 2 == 0 and height % block == 0
    scaling = 1.0 / math.sqrt(pixels * height * cols)
    span = TAPS + (-TAPS) % SUB
    vmem = pl.BlockSpec(memory_space=pltpu.VMEM)
    hbm = pl.BlockSpec(memory_space=pltpu.HBM)
    bf16, f32 = jnp.bfloat16, jnp.float32
    shapes = (
        jax.ShapeDtypeStruct((part, height, cols), bf16),
        jax.ShapeDtypeStruct((rows, cols), f32),
        jax.ShapeDtypeStruct((part, WIDE * WIDE), f32),
    )
    results = pl.pallas_call(
        functools.partial(kernel, n, chunks, scaling),
        out_shape=shapes,
        in_specs=[hbm] * 4,
        out_specs=(vmem, vmem, vmem),
        scratch_shapes=[
            pltpu.VMEM((rows, cols, pixels), bf16),
            pltpu.VMEM((pixels, pixels), bf16),
            pltpu.VMEM((1, pixels), jnp.int32),
            pltpu.VMEM((2, pixels), jnp.int32),
            pltpu.SMEM((2, pixels), jnp.int32),
            pltpu.VMEM((pixels, pixels), bf16),
            pltpu.VMEM((pixels * rows, cols), f32),
            pltpu.VMEM((rows // 2, pixels, 2 * cols), bf16),
            pltpu.VMEM((pixels, rows, cols), bf16),
            pltpu.VMEM((chunks, n + 2, part // chunks, rows, cols), bf16),
            pltpu.VMEM((part, block, 2 * block), bf16),
            pltpu.VMEM((part, cols, cols), bf16),
            pltpu.VMEM((part, 2 * block), jnp.int32),
            pltpu.VMEM((part, cols), jnp.int32),
            pltpu.VMEM((part, 2 * block), f32),
            pltpu.VMEM((part, cols), f32),
            pltpu.VMEM((span, pixels), f32),
            pltpu.VMEM((span, pixels), f32),
            pltpu.VMEM((TAPS * span, pixels), bf16),
            pltpu.VMEM((TAPS, span + rows, cols), f32),
            pltpu.VMEM((reach, cols), f32),
            pltpu.VMEM((2, HALO, cols), f32),
            pltpu.VMEM((height, cols), bf16),
            pltpu.VMEM((height + 2 * SUB, cols), f32),
            pltpu.VMEM((WIDE * cols, height), bf16),
            pltpu.VMEM((WIDE * part * SUB, cols), f32),
            pltpu.SemaphoreType.DMA((chunks, n)),
            pltpu.SemaphoreType.DMA((chunks, n)),
            pltpu.SemaphoreType.DMA((2,)),
            pltpu.SemaphoreType.DMA((2,)),
            pltpu.SemaphoreType.DMA((n,)),
            pltpu.SemaphoreType.DMA((n,)),
            pltpu.SemaphoreType.DMA((chunks,)),
            pltpu.SemaphoreType.DMA((5,)),
        ],
        compiler_params=pltpu.CompilerParams(
            collective_id=0, has_side_effects=True, vmem_limit_bytes=48 * 1024 * 1024
        ),
    )(*(pltpu.with_memory_space_constraint(a, pltpu.HBM) for a in (data, response, pixel_ids.reshape(1, pixels), shift_bins)))
    return pl.pallas_call(
        write_out,
        out_shape=shapes,
        in_specs=[vmem] * 3,
        out_specs=(hbm, hbm, hbm),
        scratch_shapes=[pltpu.SemaphoreType.DMA((3,))],
        compiler_params=pltpu.CompilerParams(vmem_limit_bytes=8 * 1024 * 1024),
    )(*results)


def solution(mesh):
    placed = (P(("groups", "strip"), None, None), P(), P(), P())
    return jax.shard_map(
        on_device,
        mesh=mesh,
        in_specs=placed,
        out_specs=(
            P("strip", "groups", None),
            P(("groups", "strip"), None),
            P(("groups", "strip"), None),
        ),
        check_vma=False,
    )
```

```python
import functools
import math

import jax
import jax.numpy as jnp
from jax import lax
from jax.experimental import pallas as pl
from jax.experimental.pallas import tpu as pltpu
from jax.sharding import PartitionSpec as P

HALO = 16
LAGS = 4
TAPS = 2 * HALO + 1
WIDE = 2 * LAGS + 1
SUB = 8
MESH = pl.DeviceIdType.MESH


def tap_value(offset, bins):
    u = offset.astype(jnp.float32) - bins.astype(jnp.float32) / 4.0
    angle = jnp.pi * u
    safe = jnp.where(u == 0.0, 1.0, angle)
    sinc = jnp.where(u == 0.0, 1.0, jnp.sin(safe) / safe)
    value = sinc * (0.5 + 0.5 * jnp.cos(angle / (HALO + 1)))
    inside = (jnp.abs(u) < HALO + 1) & (jnp.abs(offset) <= HALO)
    return jnp.where(inside, value, 0.0).astype(jnp.bfloat16)


def kernel(
    n, chunks, scaling,
    data_hbm, resp_hbm, ids_hbm, bins_hbm,
    aligned_ref, sum_ref, corr_out_ref,
    data_ref, resp_ref, ids_ref, bins_ref, bins_smem,
    chosen_t, spread, natural, corrected, received, row_bands, col_bands, row_bins, col_bins,
    row_lines, col_lines, row_taps, col_taps, outer_taps,
    totals, halo_out, halo_in, image, image_pad, image_t, diagonals,
    send_sems, recv_sems, halo_send, halo_recv, image_send, image_recv, own_sem, load_sems,
):
    rows, cols, pixels = data_ref.shape
    half_rows = rows // 2
    part = pixels // n
    size = part // chunks
    height = n * rows
    block = min(128, height)
    reach = rows + 2 * HALO
    span = TAPS + (-TAPS) % SUB
    me = lax.axis_index("strip")
    flat_loop = n <= 16

    loads = [
        pltpu.make_async_copy(source, target, load_sems.at[k])
        for k, (source, target) in enumerate(
            (
                (resp_hbm, resp_ref),
                (ids_hbm, ids_ref),
                (data_hbm, data_ref),
                (bins_hbm, bins_ref),
                (bins_hbm, bins_smem),
            )
        )
    ]
    for load in loads:
        load.start()

    barrier = pltpu.get_barrier_semaphore()

    def greet(t, carry):
        other = lax.rem(me + t, n)
        pl.semaphore_signal(barrier, inc=1, device_id={"strip": other}, device_id_type=MESH)
        return carry

    lax.fori_loop(1, n, greet, 0, unroll=flat_loop)

    loads[0].wait()
    loads[1].wait()
    pick = lax.broadcasted_iota(jnp.int32, (pixels, pixels), 0) == ids_ref[...]
    chosen = jnp.dot(
        resp_ref[...], pick.astype(jnp.float32).astype(jnp.bfloat16), preferred_element_type=jnp.float32
    )
    chosen_t[...] = chosen.T.astype(jnp.bfloat16)
    loads[2].wait()

    def correct(first, count):
        first = pl.multiple_of(first, 16)
        for y in range(half_rows):
            both_rows = jnp.concatenate([data_ref[y], data_ref[y + half_rows]], axis=0)
            pair_rows = lax.dot_general(
                chosen_t[pl.ds(first, count), :],
                both_rows,
                (((1,), (1,)), ((), ())),
                preferred_element_type=jnp.float32,
            )
            natural[y, pl.ds(first, count), :] = pair_rows.astype(jnp.bfloat16)
            spread[pl.ds(first * rows + y, count, stride=rows), :] = pair_rows[:, :cols]
            spread[pl.ds(first * rows + y + half_rows, count, stride=rows), :] = pair_rows[:, cols:]
        flat = spread[pl.ds(pl.multiple_of(first * rows, 16), count * rows), :]
        corrected[pl.ds(first, count)] = flat.reshape(count, rows, cols).astype(jnp.bfloat16)

    def strip_copy(chunk, other, owner, sender):
        return pltpu.make_async_remote_copy(
            src_ref=corrected.at[pl.ds(owner * part + chunk * size, size)],
            dst_ref=received.at[chunk, sender + 1],
            send_sem=send_sems.at[chunk, other],
            recv_sem=recv_sems.at[chunk, sender],
            device_id={"strip": other},
            device_id_type=MESH,
        )

    def partner(step):
        half = lax.div(step + 1, 2)
        even = lax.rem(step, 2) == 0
        if n & (n - 1):
            return lax.rem(me + n // 2 + jnp.where(even, half, -half), n)
        return me ^ jnp.where(even, n // 2 + half, half)

    def send_chunk(chunk):
        def one(step, carry):
            other = partner(step)
            strip_copy(chunk, other, other, me).start()
            return carry

        lax.fori_loop(0, n - 1, one, 0, unroll=flat_loop)

    def await_left(chunk):
        def one(step, carry):
            other = partner(step)
            strip_copy(chunk, other, other, me).wait_send()
            return carry

        lax.fori_loop(0, n - 1, one, 0, unroll=flat_loop)

    early = 1
    if n & (n - 1) or n < 4:
        correct(0, pixels)
        pl.semaphore_wait(barrier, n - 1)
        for chunk in range(early):
            send_chunk(chunk)
    else:
        side = lax.div(me, n // 2)
        correct((1 - side) * (pixels // 2), pixels // 2)
        pl.semaphore_wait(barrier, n - 1)

        def send_far(step, carry):
            other = me ^ (n // 2 + step)
            strip_copy(0, other, other, me).start()
            return carry

        def send_near(step, carry):
            other = me ^ step
            strip_copy(0, other, other, me).start()
            return carry

        lax.fori_loop(0, n // 2, send_far, 0, unroll=flat_loop)
        correct(side * (pixels // 2), pixels // 2)
        lax.fori_loop(1, n // 2, send_near, 0, unroll=flat_loop)
        for chunk in range(1, early):
            send_chunk(chunk)
    own_copies = [
        pltpu.make_async_copy(
            corrected.at[pl.ds(me * part + chunk * size, size)],
            received.at[chunk, me + 1],
            own_sem.at[chunk],
        )
        for chunk in range(chunks)
    ]
    for own_copy in own_copies:
        own_copy.start()

    loads[3].wait()
    loads[4].wait()
    taps_at = lax.broadcasted_iota(jnp.int32, (span, pixels), 0) - HALO
    row_taps[...] = tap_value(taps_at, bins_ref[0:1, :]).astype(jnp.float32)
    col_taps[...] = tap_value(taps_at, bins_ref[1:2, :]).astype(jnp.float32)
    totals[...] = jnp.zeros_like(totals)
    outer = row_taps[...].reshape(1, span, pixels) * col_taps[pl.ds(0, TAPS), :].reshape(TAPS, 1, pixels)
    outer_taps[...] = outer.reshape(TAPS * span, pixels).astype(jnp.bfloat16)
    gap = jnp.zeros((TAPS, half_rows, cols), jnp.float32)
    for y in range(half_rows):
        terms = jnp.dot(outer_taps[...], natural[y], preferred_element_type=jnp.float32)
        terms = terms.reshape(TAPS, span, 2 * cols)
        terms = jnp.concatenate([terms[:, :, :cols], gap], axis=1) + jnp.concatenate(
            [gap, terms[:, :, cols:]], axis=1
        )
        totals[:, pl.ds(y, span + half_rows), :] += terms
    lane = lax.broadcasted_iota(jnp.int32, (reach, cols), 1)
    share = jnp.zeros((reach, cols), jnp.float32)
    for j in range(TAPS):
        shift = j - HALO
        moved = totals[j, pl.ds(0, reach), :]
        if shift:
            moved = pltpu.roll(moved, shift % cols, 1)
            source = lane - shift
            moved = jnp.where((source >= 0) & (source < cols), moved, 0.0)
        share = share + moved
    halo_out[...] = share

    before, after = lax.rem(me + n - 1, n), lax.rem(me + 1, n)

    def halo_copy(side, other, start):
        return pltpu.make_async_remote_copy(
            src_ref=halo_out.at[pl.ds(start, HALO)],
            dst_ref=halo_in.at[side],
            send_sem=halo_send.at[side],
            recv_sem=halo_recv.at[side],
            device_id={"strip": other},
            device_id_type=MESH,
        )

    to_after = halo_copy(0, after, HALO + rows)
    to_before = halo_copy(1, before, 0)
    to_after.start()
    to_before.start()
    middle = min(2, chunks)
    late = min(3, chunks)
    for chunk in range(early, middle):
        send_chunk(chunk)
    for i in range(part):
        row_bins[pl.ds(i, 1), :] = jnp.full((1, 2 * block), bins_smem[0, me * part + i], jnp.int32)
        col_bins[pl.ds(i, 1), :] = jnp.full((1, cols), bins_smem[1, me * part + i], jnp.int32)
    band_lane = lax.broadcasted_iota(jnp.int32, (part, 2 * block), 1)
    col_lane = lax.broadcasted_iota(jnp.int32, (part, cols), 1)
    col_offset = jnp.where(col_lane < cols // 2, col_lane, col_lane - cols)
    row_lines[...] = tap_value(HALO - band_lane, row_bins[...]).astype(jnp.float32)
    col_lines[...] = tap_value(col_offset, col_bins[...]).astype(jnp.float32)
    square = (cols, cols)
    near = (
        jnp.abs(lax.broadcasted_iota(jnp.int32, square, 0) - lax.broadcasted_iota(jnp.int32, square, 1))
        <= HALO
    )

    def bands(i, carry):
        row_band = jnp.broadcast_to(row_lines[pl.ds(i, 1), :], (block, 2 * block))
        row_bands[i] = pltpu.roll(row_band, 0, 1, stride=1, stride_axis=0).astype(jnp.bfloat16)
        col_band = jnp.broadcast_to(col_lines[pl.ds(i, 1), :], square)
        col_band = pltpu.roll(col_band, 0, 1, stride=1, stride_axis=0)
        col_bands[i] = jnp.where(near, col_band, 0.0).astype(jnp.bfloat16)
        return carry

    lax.fori_loop(0, part, bands, 0)
    edge = jnp.zeros((chunks, size, rows, cols), jnp.bfloat16)
    received[:, 0] = edge
    received[:, n + 1] = edge

    to_after.wait_recv()
    to_before.wait_recv()
    mine = halo_out[pl.ds(HALO, rows), :]
    fill = jnp.zeros((rows - HALO, cols), jnp.float32)
    from_before = jnp.where(me > 0, halo_in[0], 0.0)
    from_after = jnp.where(me < n - 1, halo_in[1], 0.0)
    if rows > HALO:
        from_before = jnp.concatenate([from_before, fill], axis=0)
        from_after = jnp.concatenate([fill, from_after], axis=0)
    mine = mine + from_before + from_after
    sum_ref[...] = mine
    image[pl.ds(pl.multiple_of(me * rows, HALO), rows), :] = mine.astype(jnp.bfloat16)

    def image_copy(other, sender):
        place = pl.ds(pl.multiple_of(sender * rows, HALO), rows)
        return pltpu.make_async_remote_copy(
            src_ref=image.at[place],
            dst_ref=image.at[place],
            send_sem=image_send.at[other],
            recv_sem=image_recv.at[sender],
            device_id={"strip": other},
            device_id_type=MESH,
        )

    def send_image(step, carry):
        image_copy(partner(step), me).start()
        return carry

    lax.fori_loop(0, n - 1, send_image, 0, unroll=flat_loop)
    for chunk in range(middle, late):
        send_chunk(chunk)

    def align(chunk):
        def await_strip(step, inner):
            other = lax.rem(me + step, n)
            strip_copy(chunk, other, other, other).wait_recv()
            return inner

        lax.fori_loop(1, n, await_strip, 0, unroll=flat_loop)

        def one(index, inner):
            i = chunk * size + index
            row_band = row_bands[i][:, : block + 2 * HALO]
            col_band = col_bands[i]
            for start in range(0, height, block):
                window = received[chunk, pl.ds(start // rows, block // rows + 2), index]
                window = window.reshape(block + 2 * rows, cols)[rows - HALO : rows + block + HALO]
                moved = jnp.dot(row_band, window, preferred_element_type=jnp.float32)
                moved = jnp.dot(
                    moved.astype(jnp.bfloat16), col_band, preferred_element_type=jnp.float32
                )
                aligned_ref[i, pl.ds(start, block), :] = moved.astype(jnp.bfloat16)
            return inner

        lax.fori_loop(0, size, one, 0, unroll=True)

    for own_copy in own_copies:
        own_copy.wait()
    align(0)
    for chunk in range(late, chunks):
        await_left(chunk - 2)
        send_chunk(chunk)

    def await_image(step, carry):
        other = lax.rem(me + step, n)
        image_copy(other, other).wait_recv()
        return carry

    lax.fori_loop(1, n, await_image, 0, unroll=flat_loop)
    image_pad[pl.ds(0, SUB), :] = jnp.zeros((SUB, cols), jnp.float32)
    image_pad[pl.ds(SUB + height, SUB), :] = jnp.zeros((SUB, cols), jnp.float32)
    image_pad[pl.ds(SUB, height), :] = image[...].astype(jnp.float32)
    for a in range(WIDE):
        window = image_pad[pl.ds(SUB + a - LAGS, height), :]
        image_t[pl.ds(a * cols, cols), :] = window.T.astype(jnp.bfloat16)

    low_lane = lax.broadcasted_iota(jnp.int32, (SUB, cols), 1) < cols // 2
    tail_lane = lax.broadcasted_iota(jnp.int32, (SUB, cols), 1)
    tail_keep = (tail_lane < SUB) | (tail_lane >= cols // 2)
    pieces = cols // SUB

    def correlate(chunk):
        def pair(index, inner):
            first = chunk * size + 2 * index
            both = jnp.concatenate([aligned_ref[first], aligned_ref[first + 1]], axis=1)
            for a in range(WIDE):
                products = jnp.dot(
                    image_t[pl.ds(a * cols, cols), :], both, preferred_element_type=jnp.float32
                )
                for k in range(2):
                    total = None
                    for piece in range(pieces):
                        term = products[piece * SUB : (piece + 1) * SUB, k * cols : (k + 1) * cols]
                        if piece:
                            term = pltpu.roll(term, cols - piece * SUB, 1)
                        if piece == 0:
                            term = jnp.where(low_lane, term, 0.0)
                        elif piece == pieces - 1:
                            term = jnp.where(tail_keep, term, 0.0)
                        total = term if total is None else total + term
                    place = pl.multiple_of((a * part + first + k) * SUB, SUB)
                    diagonals[pl.ds(place, SUB), :] = total
            return inner

        lax.fori_loop(0, size // 2, pair, 0)

    correlate(0)

    def drain(step, carry):
        image_copy(lax.rem(me + step, n), me).wait_send()
        return carry

    lax.fori_loop(1, n, drain, 0, unroll=flat_loop)
    to_after.wait_send()
    to_before.wait_send()
    left = set(range(late - 2, chunks - 2)) if chunks > late else set()
    for chunk in range(1, chunks):
        if chunk - 1 not in left:
            await_left(chunk - 1)
            left.add(chunk - 1)
        align(chunk)
        correlate(chunk)

    gathered = jnp.zeros((WIDE * part, cols), jnp.float32)
    for s in range(SUB):
        lines = diagonals[pl.ds(s, WIDE * part, stride=SUB), :]
        turn = (LAGS - s) % cols
        gathered = gathered + (pltpu.roll(lines, turn, 1) if turn else lines)
    lane_in = lax.broadcasted_iota(jnp.int32, square, 0)
    lane_out = lax.broadcasted_iota(jnp.int32, square, 1)
    mirror = ((lane_in + lane_out == 2 * LAGS) & (lane_out < WIDE)).astype(jnp.float32)
    gathered = jnp.dot(
        gathered, mirror, precision=lax.Precision.HIGHEST, preferred_element_type=jnp.float32
    )
    result = jnp.zeros((part, cols), jnp.float32)
    for a in range(WIDE):
        lags = gathered[a * part : (a + 1) * part, :]
        result = result + (pltpu.roll(lags, a * WIDE, 1) if a else lags)
    corr_out_ref[...] = (result * scaling)[:, : WIDE * WIDE]

    if chunks - 1 not in left:
        await_left(chunks - 1)


def write_out(*refs):
    copies = [pltpu.make_async_copy(refs[k], refs[3 + k], refs[6].at[k]) for k in range(3)]
    for copy in copies:
        copy.start()
    for copy in copies:
        copy.wait()


def on_device(data, response, pixel_ids, shift_bins):
    rows, cols, pixels = data.shape
    n = lax.axis_size("strip")
    part = pixels // n
    chunks = max(1, part // 4)
    height = n * rows
    block = min(128, height)
    reach = rows + 2 * HALO
    assert rows >= HALO and rows % 16 == 0 and block % rows == 0 and (part // chunks) % 2 == 0 and height % block == 0
    scaling = 1.0 / math.sqrt(pixels * height * cols)
    span = TAPS + (-TAPS) % SUB
    vmem = pl.BlockSpec(memory_space=pltpu.VMEM)
    hbm = pl.BlockSpec(memory_space=pltpu.HBM)
    bf16, f32 = jnp.bfloat16, jnp.float32
    shapes = (
        jax.ShapeDtypeStruct((part, height, cols), bf16),
        jax.ShapeDtypeStruct((rows, cols), f32),
        jax.ShapeDtypeStruct((part, WIDE * WIDE), f32),
    )
    results = pl.pallas_call(
        functools.partial(kernel, n, chunks, scaling),
        out_shape=shapes,
        in_specs=[hbm] * 4,
        out_specs=(vmem, vmem, vmem),
        scratch_shapes=[
            pltpu.VMEM((rows, cols, pixels), bf16),
            pltpu.VMEM((pixels, pixels), bf16),
            pltpu.VMEM((1, pixels), jnp.int32),
            pltpu.VMEM((2, pixels), jnp.int32),
            pltpu.SMEM((2, pixels), jnp.int32),
            pltpu.VMEM((pixels, pixels), bf16),
            pltpu.VMEM((pixels * rows, cols), f32),
            pltpu.VMEM((rows // 2, pixels, 2 * cols), bf16),
            pltpu.VMEM((pixels, rows, cols), bf16),
            pltpu.VMEM((chunks, n + 2, part // chunks, rows, cols), bf16),
            pltpu.VMEM((part, block, 2 * block), bf16),
            pltpu.VMEM((part, cols, cols), bf16),
            pltpu.VMEM((part, 2 * block), jnp.int32),
            pltpu.VMEM((part, cols), jnp.int32),
            pltpu.VMEM((part, 2 * block), f32),
            pltpu.VMEM((part, cols), f32),
            pltpu.VMEM((span, pixels), f32),
            pltpu.VMEM((span, pixels), f32),
            pltpu.VMEM((TAPS * span, pixels), bf16),
            pltpu.VMEM((TAPS, span + rows, cols), f32),
            pltpu.VMEM((reach, cols), f32),
            pltpu.VMEM((2, HALO, cols), f32),
            pltpu.VMEM((height, cols), bf16),
            pltpu.VMEM((height + 2 * SUB, cols), f32),
            pltpu.VMEM((WIDE * cols, height), bf16),
            pltpu.VMEM((WIDE * part * SUB, cols), f32),
            pltpu.SemaphoreType.DMA((chunks, n)),
            pltpu.SemaphoreType.DMA((chunks, n)),
            pltpu.SemaphoreType.DMA((2,)),
            pltpu.SemaphoreType.DMA((2,)),
            pltpu.SemaphoreType.DMA((n,)),
            pltpu.SemaphoreType.DMA((n,)),
            pltpu.SemaphoreType.DMA((chunks,)),
            pltpu.SemaphoreType.DMA((5,)),
        ],
        compiler_params=pltpu.CompilerParams(
            collective_id=0, has_side_effects=True, vmem_limit_bytes=48 * 1024 * 1024
        ),
    )(*(pltpu.with_memory_space_constraint(a, pltpu.HBM) for a in (data, response, pixel_ids.reshape(1, pixels), shift_bins)))
    return pl.pallas_call(
        write_out,
        out_shape=shapes,
        in_specs=[vmem] * 3,
        out_specs=(hbm, hbm, hbm),
        scratch_shapes=[pltpu.SemaphoreType.DMA((3,))],
        compiler_params=pltpu.CompilerParams(vmem_limit_bytes=8 * 1024 * 1024),
    )(*results)


def solution(mesh):
    placed = (P(("groups", "strip"), None, None), P(), P(), P())
    return jax.shard_map(
        on_device,
        mesh=mesh,
        in_specs=placed,
        out_specs=(
            P("strip", "groups", None),
            P(("groups", "strip"), None),
            P(("groups", "strip"), None),
        ),
        check_vma=False,
    )
```

```python
import functools
import math

import jax
import jax.numpy as jnp
from jax import lax
from jax.experimental import pallas as pl
from jax.experimental.pallas import tpu as pltpu
from jax.sharding import PartitionSpec as P

HALO = 16
LAGS = 4
TAPS = 2 * HALO + 1
WIDE = 2 * LAGS + 1
SUB = 8
MESH = pl.DeviceIdType.MESH


def tap_value(offset, bins):
    u = offset.astype(jnp.float32) - bins.astype(jnp.float32) / 4.0
    angle = jnp.pi * u
    safe = jnp.where(u == 0.0, 1.0, angle)
    sinc = jnp.where(u == 0.0, 1.0, jnp.sin(safe) / safe)
    value = sinc * (0.5 + 0.5 * jnp.cos(angle / (HALO + 1)))
    inside = (jnp.abs(u) < HALO + 1) & (jnp.abs(offset) <= HALO)
    return jnp.where(inside, value, 0.0).astype(jnp.bfloat16)


def kernel(
    n, sizes, scaling,
    data_hbm, resp_hbm, ids_hbm, bins_hbm,
    aligned_ref, sum_ref, corr_out_ref,
    data_ref, resp_ref, ids_ref, bins_ref, bins_smem,
    chosen_t, spread, natural, corrected, received, row_bands, col_bands, row_bins, col_bins,
    row_lines, col_lines, row_taps, col_taps, outer_taps,
    totals, halo_out, halo_in, image, image_pad, image_t, diagonals,
    send_sems, recv_sems, halo_send, halo_recv, image_send, image_recv, own_sem, load_sems,
):
    rows, cols, pixels = data_ref.shape
    half_rows = rows // 2
    part = pixels // n
    chunks = len(sizes)
    firsts = [sum(sizes[:k]) for k in range(chunks)]
    height = n * rows
    block = min(128, height)
    reach = rows + 2 * HALO
    span = TAPS + (-TAPS) % SUB
    me = lax.axis_index("strip")
    flat_loop = n <= 16

    loads = [
        pltpu.make_async_copy(source, target, load_sems.at[k])
        for k, (source, target) in enumerate(
            (
                (resp_hbm, resp_ref),
                (ids_hbm, ids_ref),
                (data_hbm, data_ref),
                (bins_hbm, bins_ref),
                (bins_hbm, bins_smem),
            )
        )
    ]
    for load in loads:
        load.start()

    barrier = pltpu.get_barrier_semaphore()

    def greet(t, carry):
        other = lax.rem(me + t, n)
        pl.semaphore_signal(barrier, inc=1, device_id={"strip": other}, device_id_type=MESH)
        return carry

    lax.fori_loop(1, n, greet, 0, unroll=flat_loop)

    loads[0].wait()
    loads[1].wait()
    pick = lax.broadcasted_iota(jnp.int32, (pixels, pixels), 0) == ids_ref[...]
    chosen = jnp.dot(
        resp_ref[...], pick.astype(jnp.float32).astype(jnp.bfloat16), preferred_element_type=jnp.float32
    )
    chosen_t[...] = chosen.T.astype(jnp.bfloat16)
    loads[2].wait()

    def correct(first, count):
        first = pl.multiple_of(first, 16)
        for y in range(half_rows):
            both_rows = jnp.concatenate([data_ref[y], data_ref[y + half_rows]], axis=0)
            pair_rows = lax.dot_general(
                chosen_t[pl.ds(first, count), :],
                both_rows,
                (((1,), (1,)), ((), ())),
                preferred_element_type=jnp.float32,
            )
            natural[y, pl.ds(first, count), :] = pair_rows.astype(jnp.bfloat16)
            spread[pl.ds(first * rows + y, count, stride=rows), :] = pair_rows[:, :cols]
            spread[pl.ds(first * rows + y + half_rows, count, stride=rows), :] = pair_rows[:, cols:]
        flat = spread[pl.ds(pl.multiple_of(first * rows, 16), count * rows), :]
        corrected[pl.ds(first, count)] = flat.reshape(count, rows, cols).astype(jnp.bfloat16)

    def strip_copy(chunk, other, owner, sender):
        return pltpu.make_async_remote_copy(
            src_ref=corrected.at[pl.ds(owner * part + firsts[chunk], sizes[chunk])],
            dst_ref=received[chunk].at[sender + 1],
            send_sem=send_sems.at[chunk, other],
            recv_sem=recv_sems.at[chunk, sender],
            device_id={"strip": other},
            device_id_type=MESH,
        )

    def partner(step):
        half = lax.div(step + 1, 2)
        even = lax.rem(step, 2) == 0
        if n & (n - 1):
            return lax.rem(me + n // 2 + jnp.where(even, half, -half), n)
        return me ^ jnp.where(even, n // 2 + half, half)

    def send_chunk(chunk):
        def one(step, carry):
            other = partner(step)
            strip_copy(chunk, other, other, me).start()
            return carry

        lax.fori_loop(0, n - 1, one, 0, unroll=flat_loop)

    def await_left(chunk):
        def one(step, carry):
            other = partner(step)
            strip_copy(chunk, other, other, me).wait_send()
            return carry

        lax.fori_loop(0, n - 1, one, 0, unroll=flat_loop)

    early = 1
    if n & (n - 1) or n < 4:
        correct(0, pixels)
        pl.semaphore_wait(barrier, n - 1)
        for chunk in range(early):
            send_chunk(chunk)
    else:
        side = lax.div(me, n // 2)
        correct((1 - side) * (pixels // 2), pixels // 2)
        pl.semaphore_wait(barrier, n - 1)

        def send_far(step, carry):
            other = me ^ (n // 2 + step)
            strip_copy(0, other, other, me).start()
            return carry

        def send_near(step, carry):
            other = me ^ step
            strip_copy(0, other, other, me).start()
            return carry

        lax.fori_loop(0, n // 2, send_far, 0, unroll=flat_loop)
        correct(side * (pixels // 2), pixels // 2)
        lax.fori_loop(1, n // 2, send_near, 0, unroll=flat_loop)
        for chunk in range(1, early):
            send_chunk(chunk)
    own_copies = [
        pltpu.make_async_copy(
            corrected.at[pl.ds(me * part + firsts[chunk], sizes[chunk])],
            received[chunk].at[me + 1],
            own_sem.at[chunk],
        )
        for chunk in range(chunks)
    ]
    for own_copy in own_copies:
        own_copy.start()

    loads[3].wait()
    loads[4].wait()
    taps_at = lax.broadcasted_iota(jnp.int32, (span, pixels), 0) - HALO
    row_taps[...] = tap_value(taps_at, bins_ref[0:1, :]).astype(jnp.float32)
    col_taps[...] = tap_value(taps_at, bins_ref[1:2, :]).astype(jnp.float32)
    totals[...] = jnp.zeros_like(totals)
    outer = row_taps[...].reshape(1, span, pixels) * col_taps[pl.ds(0, TAPS), :].reshape(TAPS, 1, pixels)
    outer_taps[...] = outer.reshape(TAPS * span, pixels).astype(jnp.bfloat16)
    gap = jnp.zeros((TAPS, half_rows, cols), jnp.float32)
    for y in range(half_rows):
        terms = jnp.dot(outer_taps[...], natural[y], preferred_element_type=jnp.float32)
        terms = terms.reshape(TAPS, span, 2 * cols)
        terms = jnp.concatenate([terms[:, :, :cols], gap], axis=1) + jnp.concatenate(
            [gap, terms[:, :, cols:]], axis=1
        )
        totals[:, pl.ds(y, span + half_rows), :] += terms
    lane = lax.broadcasted_iota(jnp.int32, (reach, cols), 1)
    share = jnp.zeros((reach, cols), jnp.float32)
    for j in range(TAPS):
        shift = j - HALO
        moved = totals[j, pl.ds(0, reach), :]
        if shift:
            moved = pltpu.roll(moved, shift % cols, 1)
            source = lane - shift
            moved = jnp.where((source >= 0) & (source < cols), moved, 0.0)
        share = share + moved
    halo_out[...] = share

    before, after = lax.rem(me + n - 1, n), lax.rem(me + 1, n)

    def halo_copy(side, other, start):
        return pltpu.make_async_remote_copy(
            src_ref=halo_out.at[pl.ds(start, HALO)],
            dst_ref=halo_in.at[side],
            send_sem=halo_send.at[side],
            recv_sem=halo_recv.at[side],
            device_id={"strip": other},
            device_id_type=MESH,
        )

    to_after = halo_copy(0, after, HALO + rows)
    to_before = halo_copy(1, before, 0)
    to_after.start()
    to_before.start()
    middle = min(2, chunks)
    late = min(3, chunks)
    for chunk in range(early, middle):
        send_chunk(chunk)
    for i in range(part):
        row_bins[pl.ds(i, 1), :] = jnp.full((1, 2 * block), bins_smem[0, me * part + i], jnp.int32)
        col_bins[pl.ds(i, 1), :] = jnp.full((1, cols), bins_smem[1, me * part + i], jnp.int32)
    band_lane = lax.broadcasted_iota(jnp.int32, (part, 2 * block), 1)
    col_lane = lax.broadcasted_iota(jnp.int32, (part, cols), 1)
    col_offset = jnp.where(col_lane < cols // 2, col_lane, col_lane - cols)
    row_lines[...] = tap_value(HALO - band_lane, row_bins[...]).astype(jnp.float32)
    col_lines[...] = tap_value(col_offset, col_bins[...]).astype(jnp.float32)
    square = (cols, cols)
    near = (
        jnp.abs(lax.broadcasted_iota(jnp.int32, square, 0) - lax.broadcasted_iota(jnp.int32, square, 1))
        <= HALO
    )

    def bands(i, carry):
        row_band = jnp.broadcast_to(row_lines[pl.ds(i, 1), :], (block, 2 * block))
        row_bands[i] = pltpu.roll(row_band, 0, 1, stride=1, stride_axis=0).astype(jnp.bfloat16)
        col_band = jnp.broadcast_to(col_lines[pl.ds(i, 1), :], square)
        col_band = pltpu.roll(col_band, 0, 1, stride=1, stride_axis=0)
        col_bands[i] = jnp.where(near, col_band, 0.0).astype(jnp.bfloat16)
        return carry

    lax.fori_loop(0, part, bands, 0)
    for chunk in range(chunks):
        edge = jnp.zeros((sizes[chunk], rows, cols), jnp.bfloat16)
        received[chunk][0] = edge
        received[chunk][n + 1] = edge

    to_after.wait_recv()
    to_before.wait_recv()
    mine = halo_out[pl.ds(HALO, rows), :]
    fill = jnp.zeros((rows - HALO, cols), jnp.float32)
    from_before = jnp.where(me > 0, halo_in[0], 0.0)
    from_after = jnp.where(me < n - 1, halo_in[1], 0.0)
    if rows > HALO:
        from_before = jnp.concatenate([from_before, fill], axis=0)
        from_after = jnp.concatenate([fill, from_after], axis=0)
    mine = mine + from_before + from_after
    sum_ref[...] = mine
    image[pl.ds(pl.multiple_of(me * rows, HALO), rows), :] = mine.astype(jnp.bfloat16)

    def image_copy(other, sender):
        place = pl.ds(pl.multiple_of(sender * rows, HALO), rows)
        return pltpu.make_async_remote_copy(
            src_ref=image.at[place],
            dst_ref=image.at[place],
            send_sem=image_send.at[other],
            recv_sem=image_recv.at[sender],
            device_id={"strip": other},
            device_id_type=MESH,
        )

    def send_image(step, carry):
        image_copy(partner(step), me).start()
        return carry

    lax.fori_loop(0, n - 1, send_image, 0, unroll=flat_loop)
    for chunk in range(middle, late):
        send_chunk(chunk)

    def align(chunk):
        def await_strip(step, inner):
            other = lax.rem(me + step, n)
            strip_copy(chunk, other, other, other).wait_recv()
            return inner

        lax.fori_loop(1, n, await_strip, 0, unroll=flat_loop)

        def one(index, inner):
            i = firsts[chunk] + index
            row_band = row_bands[i][:, : block + 2 * HALO]
            col_band = col_bands[i]
            for start in range(0, height, block):
                window = received[chunk][pl.ds(start // rows, block // rows + 2), index]
                window = window.reshape(block + 2 * rows, cols)[rows - HALO : rows + block + HALO]
                moved = jnp.dot(row_band, window, preferred_element_type=jnp.float32)
                moved = jnp.dot(
                    moved.astype(jnp.bfloat16), col_band, preferred_element_type=jnp.float32
                )
                aligned_ref[i, pl.ds(start, block), :] = moved.astype(jnp.bfloat16)
            return inner

        lax.fori_loop(0, sizes[chunk], one, 0, unroll=min(4, sizes[chunk]))

    for own_copy in own_copies:
        own_copy.wait()
    align(0)
    for chunk in range(late, chunks):
        await_left(chunk - 2)
        send_chunk(chunk)

    def await_image(step, carry):
        other = lax.rem(me + step, n)
        image_copy(other, other).wait_recv()
        return carry

    lax.fori_loop(1, n, await_image, 0, unroll=flat_loop)
    image_pad[pl.ds(0, SUB), :] = jnp.zeros((SUB, cols), jnp.float32)
    image_pad[pl.ds(SUB + height, SUB), :] = jnp.zeros((SUB, cols), jnp.float32)
    image_pad[pl.ds(SUB, height), :] = image[...].astype(jnp.float32)
    for a in range(WIDE):
        window = image_pad[pl.ds(SUB + a - LAGS, height), :]
        image_t[pl.ds(a * cols, cols), :] = window.T.astype(jnp.bfloat16)

    low_lane = lax.broadcasted_iota(jnp.int32, (SUB, cols), 1) < cols // 2
    tail_lane = lax.broadcasted_iota(jnp.int32, (SUB, cols), 1)
    tail_keep = (tail_lane < SUB) | (tail_lane >= cols // 2)
    pieces = cols // SUB

    def correlate(chunk):
        def pair(index, inner):
            first = firsts[chunk] + 2 * index
            both = jnp.concatenate([aligned_ref[first], aligned_ref[first + 1]], axis=1)
            for a in range(WIDE):
                products = jnp.dot(
                    image_t[pl.ds(a * cols, cols), :], both, preferred_element_type=jnp.float32
                )
                for k in range(2):
                    total = None
                    for piece in range(pieces):
                        term = products[piece * SUB : (piece + 1) * SUB, k * cols : (k + 1) * cols]
                        if piece:
                            term = pltpu.roll(term, cols - piece * SUB, 1)
                        if piece == 0:
                            term = jnp.where(low_lane, term, 0.0)
                        elif piece == pieces - 1:
                            term = jnp.where(tail_keep, term, 0.0)
                        total = term if total is None else total + term
                    place = pl.multiple_of((a * part + first + k) * SUB, SUB)
                    diagonals[pl.ds(place, SUB), :] = total
            return inner

        lax.fori_loop(0, sizes[chunk] // 2, pair, 0)

    correlate(0)

    def drain(step, carry):
        image_copy(lax.rem(me + step, n), me).wait_send()
        return carry

    lax.fori_loop(1, n, drain, 0, unroll=flat_loop)
    to_after.wait_send()
    to_before.wait_send()
    left = set(range(late - 2, chunks - 2)) if chunks > late else set()
    for chunk in range(1, chunks):
        if chunk - 1 not in left:
            await_left(chunk - 1)
            left.add(chunk - 1)
        align(chunk)
        correlate(chunk)

    gathered = jnp.zeros((WIDE * part, cols), jnp.float32)
    for s in range(SUB):
        lines = diagonals[pl.ds(s, WIDE * part, stride=SUB), :]
        turn = (LAGS - s) % cols
        gathered = gathered + (pltpu.roll(lines, turn, 1) if turn else lines)
    lane_in = lax.broadcasted_iota(jnp.int32, square, 0)
    lane_out = lax.broadcasted_iota(jnp.int32, square, 1)
    mirror = ((lane_in + lane_out == 2 * LAGS) & (lane_out < WIDE)).astype(jnp.float32)
    gathered = jnp.dot(
        gathered, mirror, precision=lax.Precision.HIGHEST, preferred_element_type=jnp.float32
    )
    result = jnp.zeros((part, cols), jnp.float32)
    for a in range(WIDE):
        lags = gathered[a * part : (a + 1) * part, :]
        result = result + (pltpu.roll(lags, a * WIDE, 1) if a else lags)
    corr_out_ref[...] = (result * scaling)[:, : WIDE * WIDE]

    if chunks - 1 not in left:
        await_left(chunks - 1)


def write_out(*refs):
    copies = [pltpu.make_async_copy(refs[k], refs[3 + k], refs[6].at[k]) for k in range(3)]
    for copy in copies:
        copy.start()
    for copy in copies:
        copy.wait()


def on_device(data, response, pixel_ids, shift_bins):
    rows, cols, pixels = data.shape
    n = lax.axis_size("strip")
    part = pixels // n
    quarter = part // 4
    sizes = (part,) if part < 8 else (part - 2 * quarter, quarter, quarter)
    chunks = len(sizes)
    height = n * rows
    block = min(128, height)
    reach = rows + 2 * HALO
    assert rows >= HALO and rows % 16 == 0 and block % rows == 0 and all(size % 2 == 0 for size in sizes) and height % block == 0
    scaling = 1.0 / math.sqrt(pixels * height * cols)
    span = TAPS + (-TAPS) % SUB
    vmem = pl.BlockSpec(memory_space=pltpu.VMEM)
    hbm = pl.BlockSpec(memory_space=pltpu.HBM)
    bf16, f32 = jnp.bfloat16, jnp.float32
    shapes = (
        jax.ShapeDtypeStruct((part, height, cols), bf16),
        jax.ShapeDtypeStruct((rows, cols), f32),
        jax.ShapeDtypeStruct((part, WIDE * WIDE), f32),
    )
    results = pl.pallas_call(
        functools.partial(kernel, n, sizes, scaling),
        out_shape=shapes,
        in_specs=[hbm] * 4,
        out_specs=(vmem, vmem, vmem),
        scratch_shapes=[
            pltpu.VMEM((rows, cols, pixels), bf16),
            pltpu.VMEM((pixels, pixels), bf16),
            pltpu.VMEM((1, pixels), jnp.int32),
            pltpu.VMEM((2, pixels), jnp.int32),
            pltpu.SMEM((2, pixels), jnp.int32),
            pltpu.VMEM((pixels, pixels), bf16),
            pltpu.VMEM((pixels * rows, cols), f32),
            pltpu.VMEM((rows // 2, pixels, 2 * cols), bf16),
            pltpu.VMEM((pixels, rows, cols), bf16),
            [pltpu.VMEM((n + 2, size, rows, cols), bf16) for size in sizes],
            pltpu.VMEM((part, block, 2 * block), bf16),
            pltpu.VMEM((part, cols, cols), bf16),
            pltpu.VMEM((part, 2 * block), jnp.int32),
            pltpu.VMEM((part, cols), jnp.int32),
            pltpu.VMEM((part, 2 * block), f32),
            pltpu.VMEM((part, cols), f32),
            pltpu.VMEM((span, pixels), f32),
            pltpu.VMEM((span, pixels), f32),
            pltpu.VMEM((TAPS * span, pixels), bf16),
            pltpu.VMEM((TAPS, span + rows, cols), f32),
            pltpu.VMEM((reach, cols), f32),
            pltpu.VMEM((2, HALO, cols), f32),
            pltpu.VMEM((height, cols), bf16),
            pltpu.VMEM((height + 2 * SUB, cols), f32),
            pltpu.VMEM((WIDE * cols, height), bf16),
            pltpu.VMEM((WIDE * part * SUB, cols), f32),
            pltpu.SemaphoreType.DMA((chunks, n)),
            pltpu.SemaphoreType.DMA((chunks, n)),
            pltpu.SemaphoreType.DMA((2,)),
            pltpu.SemaphoreType.DMA((2,)),
            pltpu.SemaphoreType.DMA((n,)),
            pltpu.SemaphoreType.DMA((n,)),
            pltpu.SemaphoreType.DMA((chunks,)),
            pltpu.SemaphoreType.DMA((5,)),
        ],
        compiler_params=pltpu.CompilerParams(
            collective_id=0, has_side_effects=True, vmem_limit_bytes=48 * 1024 * 1024
        ),
    )(*(pltpu.with_memory_space_constraint(a, pltpu.HBM) for a in (data, response, pixel_ids.reshape(1, pixels), shift_bins)))
    return pl.pallas_call(
        write_out,
        out_shape=shapes,
        in_specs=[vmem] * 3,
        out_specs=(hbm, hbm, hbm),
        scratch_shapes=[pltpu.SemaphoreType.DMA((3,))],
        compiler_params=pltpu.CompilerParams(vmem_limit_bytes=8 * 1024 * 1024),
    )(*results)


def solution(mesh):
    placed = (P(("groups", "strip"), None, None), P(), P(), P())
    return jax.shard_map(
        on_device,
        mesh=mesh,
        in_specs=placed,
        out_specs=(
            P("strip", "groups", None),
            P(("groups", "strip"), None),
            P(("groups", "strip"), None),
        ),
        check_vma=False,
    )
```
